32 devices in a mesh: grp: 4 (over y, core), mem: 8 (over z, x).
Axes of the slice: x: 2, y: 2, z: 4, core: 2. Of those that a mesh axis runs over, the one named last changes fastest.
Arguments:
- amplitudes: bfloat16 [4, 8, 384, 384], P('grp', 'mem'), may hold values from -6 to 6
- integrals: bfloat16 [4, 8, 384, 384], P('grp', 'mem'), may hold values from -0.3125 to 0.3125
- task_list: int32 [4, 512, 3], P('grp'), may hold values from 0 to 7
- task_counts: int32 [4, 8], P('grp'), may hold values from 1 to 64, 256 in all within a row
- owner_map: int32 [8], replicated, may hold values from 0 to 7, each once
Outputs:
- cycle: bfloat16 [4, 8, 384, 384], P('grp', 'mem')
The draws below stay inside these ranges and needn't reach their ends.
Inputs may be any that keep to these rules, and one draw needn't show every extreme that they name: `task_list`: rows 64 * e to 64 * (e + 1) - 1 of a group are executor e's task slots; every id is a tile id. `task_counts`: the counts of a group sum to 256. `owner_map`: A permutation of the tile ids.
All inputs are finite; a program needn't handle non-finite values.
Results may differ from the reference program's by a relative error of at most 0.014.
Values may be sent and summed in bfloat16 or wider, within the bound.
A program may use at most 192 MiB of HBM per device.

```python
import math
import jax
import jax.numpy as jnp
import numpy as np
from jax import lax

TILE = 384
TASK_DEV = 64
TILES = 8
LIVE_TOTAL = 256
N_GRP = 4
N_MEM = 8


def set_ends(array, rng, low, high):
    shape = array.shape
    index_at = [jax.random.randint(jax.random.fold_in(rng, axis), (), 0, shape[axis]) for axis in range(len(shape))]
    array = array.at[tuple(index_at)].set(low)
    longest = shape.index(max(shape))
    index_at[longest] = (index_at[longest] + 1) % shape[longest]
    return array.at[tuple(index_at)].set(high)


def steps_of(stream_key, shape, cuts, low, high):
    def one(position, shards_of):
        steps = jax.random.uniform(jax.random.fold_in(jax.random.fold_in(stream_key, 6), position), (shards_of,), jnp.float32, low / len(cuts), high / len(cuts))
        return jnp.repeat(jnp.exp(steps), shape[position] // shards_of).reshape((-1,) + (1,) * (len(shape) - position - 1))

    level = one(*cuts[0])
    for cut in cuts[1:]:
        level = level * one(*cut)
    return level


def profile(number_of, total, reach, slope):
    weights = [(1 << 20) // math.isqrt(rank ** slope) + 1 for rank in range(2, number_of + 1)]
    rest, holding = total - reach - (number_of - 1), [1] * (number_of - 1)
    while rest > 0:
        free = [i for i in range(number_of - 1) if holding[i] < reach]
        pool, budget = sum([weights[i] for i in free]), rest
        for i in free:
            more = min(reach - holding[i], max(1, budget * weights[i] // pool), rest)
            holding[i] = holding[i] + more
            rest = rest - more
    return np.array([reach] + holding)


def ragged(stream_key, count, total, bound, slope):
    if count == 2:
        one = jax.random.randint(stream_key, (), max(1, total - bound), min(bound, total - 1) + 1)
        return jnp.stack([one, total - one])
    tallies = jnp.asarray(profile(count, total, bound, slope), jnp.int32)
    pairs = (count - 1) // 2
    donor, taker = tallies[1:1 + 2 * pairs:2], tallies[2:2 + 2 * pairs:2]
    margin = jnp.minimum(donor - 1, bound - taker)
    passed = jax.random.randint(jax.random.fold_in(stream_key, 1), (pairs,), 0, 1 << 20) % (margin + 1)
    tallies = tallies.at[1:1 + 2 * pairs:2].set(donor - passed).at[2:2 + 2 * pairs:2].set(taker + passed)
    return tallies[jax.random.permutation(jax.random.fold_in(stream_key, 2), count)]


def centred(stream_key, extent, spread, limit, pieces=(), held_as=jnp.bfloat16):
    drawn = spread * jax.random.normal(stream_key, extent, jnp.float32)
    if pieces:
        drawn = drawn * steps_of(stream_key, extent, pieces, -0.22, 0.18)
    return jnp.clip(drawn, -limit, limit).astype(held_as)


def setup_inputs(seed: int = 0) -> dict:
    key_of = jax.random.split(jax.random.key(seed), 6)
    amplitudes = centred(key_of[0], (N_GRP, TILES, TILE, TILE), 1.0, 6.0, ((0, 4), (1, 8)))
    integrals = centred(key_of[1], (N_GRP, TILES, TILE, TILE), TILE ** -0.5, 0.3125, ((0, 4), (1, 8)))
    task_list = set_ends(jax.random.randint(key_of[2], (N_GRP, N_MEM * TASK_DEV, 3), 0, TILES), jax.random.fold_in(key_of[2], 1), 0, TILES - 1).astype(jnp.int32)
    task_counts = jax.vmap(lambda own: ragged(own, N_MEM, LIVE_TOTAL, TASK_DEV, 2))(jax.random.split(key_of[3], N_GRP)).reshape((N_GRP, N_MEM)).astype(jnp.int32)
    owner_map = jax.random.permutation(key_of[4], TILES).astype(jnp.int32)
    return dict(amplitudes=amplitudes, integrals=integrals, task_list=task_list, task_counts=task_counts, owner_map=owner_map)


def reference(amplitudes, integrals, task_list, task_counts, owner_map):
    groups = N_GRP
    members = N_MEM
    amp_float = amplitudes.astype(jnp.float32)
    transposed = amp_float.reshape(groups, members, groups, TILE // groups, TILE)
    transposed = transposed.transpose(2, 1, 0, 3, 4).reshape(groups, members, TILE, TILE)
    mixed_tiles = (2.0 * amp_float - transposed).astype(jnp.bfloat16)
    holders = jnp.take(owner_map, task_list, axis=0).astype(jnp.int32)
    holder_grid = holders.reshape(groups, members, TASK_DEV, 3)
    live_all = jnp.arange(TASK_DEV, dtype=jnp.int32)[None, None, :] < task_counts[:, :, None]

    def one_group(inputs):
        group_mixed, group_int, group_holders, group_live = inputs

        def one_executor(running, inner):
            picked, living = inner
            left_tile = jnp.take(group_mixed, picked[:, 1], axis=0).astype(jnp.float32)
            right_tile = jnp.take(group_int, picked[:, 2], axis=0).astype(jnp.float32)
            product = jnp.einsum("kxy,kyz->kxz", left_tile, right_tile, precision=lax.Precision.HIGHEST)
            product = jnp.where(living[:, None, None], product, jnp.float32(0.0))
            partial_value = jnp.zeros((members, TILE, TILE), jnp.float32).at[picked[:, 0]].add(product)
            rounded = lax.optimization_barrier(partial_value.astype(jnp.bfloat16))
            return running + rounded.astype(jnp.float32), None

        start_sum = jnp.zeros((members, TILE, TILE), jnp.float32)
        running, _ = lax.scan(one_executor, start_sum, (group_holders, group_live))
        return running.astype(jnp.bfloat16)

    return lax.map(one_group, (mixed_tiles, integrals, holder_grid, live_all))
```

```python
import functools
import math

import jax
import jax.numpy as jnp
from jax import lax
from jax.experimental import pallas as pl
from jax.experimental.pallas import tpu as pltpu
from jax.sharding import PartitionSpec as P

TASK_DEV = 64


def block_products(got_mixed, got_int, picked, living):
    left_tile = jnp.take(got_mixed, picked[:, 1], axis=0)
    right_tile = jnp.take(got_int, picked[:, 2], axis=0)
    product = jnp.einsum("kxy,kyz->kxz", left_tile, right_tile, preferred_element_type=jnp.float32)
    return jnp.where(living[:, None, None], product, jnp.float32(0.0))


def add_targets(running, targets, living, product):
    safe_targets = jnp.where(living, targets, 0)
    return running.at[safe_targets].add(product)


def local(amplitudes, integrals, task_list, task_counts, owner_map):
    tile_order = amplitudes.shape[-1]
    members = lax.axis_size("mem")
    device = lax.axis_index("mem")
    slot_count = TASK_DEV
    own_amp = amplitudes[0, 0]
    swapped = lax.all_to_all(own_amp, "grp", split_axis=0, concat_axis=0, tiled=True)
    mixed_tile = (2.0 * own_amp.astype(jnp.float32) - swapped.astype(jnp.float32)).astype(
        jnp.bfloat16
    )
    own_int = integrals[0, 0]
    holders = jnp.take(owner_map, task_list[0], axis=0)
    live_all = jnp.arange(slot_count, dtype=jnp.int32)[None, :] < task_counts[0][:, None]
    got_mixed, got_int = (
        lax.all_gather(mixed_tile[None], "mem", axis=0, tiled=True),
        lax.all_gather(own_int[None], "mem", axis=0, tiled=True),
    )
    flat_live = live_all.reshape(-1)
    mine = flat_live & (holders[:, 0] == device)
    order = jnp.argsort(jnp.where(mine, 0, 1).astype(jnp.int32), stable=True)
    total_mine = jnp.sum(mine.astype(jnp.int32))
    block_size = math.gcd(members * slot_count, 16)
    block_count = (total_mine + block_size - 1) // block_size
    slot_index = jnp.arange(block_size, dtype=jnp.int32)

    def owner_step(state):
        turn, per_exec = state
        first = turn * block_size
        chosen = lax.dynamic_slice_in_dim(order, first, block_size, 0)
        picked = jnp.take(holders, chosen, axis=0)
        living = slot_index + first < total_mine
        product = block_products(got_mixed, got_int, picked, living)
        return (turn + 1, add_targets(per_exec, chosen // slot_count, living, product))

    start_exec = jnp.zeros((members, tile_order, tile_order), jnp.float32)
    _, per_exec = lax.while_loop(
        lambda state: state[0] < block_count, owner_step, (jnp.int32(0), start_exec)
    )
    summed = jnp.sum(per_exec.astype(jnp.bfloat16), axis=0, dtype=jnp.float32)
    return summed.astype(jnp.bfloat16)[None, None]


MESH = pl.DeviceIdType.MESH
STEP = 128


def remote(src, dst, send_sem, recv_sem, **place):
    return pltpu.make_async_remote_copy(
        src_ref=src, dst_ref=dst, send_sem=send_sem, recv_sem=recv_sem,
        device_id=place, device_id_type=MESH,
    )


def count_tasks(members, tasks, counts, owner):
    total = tasks.shape[-1]
    slots = total // members
    ids = [tasks[field] for field in range(3)]
    rows = [jnp.zeros((1, total), jnp.int32) for _ in range(3)]
    for tile_id in range(members):
        row = owner[tile_id]
        rows = [jnp.where(ids[f] == tile_id, row, rows[f]) for f in range(3)]
    place = lax.broadcasted_iota(jnp.int32, (1, total), 1)
    live = jnp.zeros((1, total), jnp.int32)
    for executor in range(members):
        offset = place - executor * slots
        inside = (offset >= 0) & (offset < jnp.minimum(counts[0, executor], slots))
        live = jnp.where(inside, 1, live)
    target = jnp.where(live == 1, rows[0], -1)
    pair = rows[1] * members + rows[2]
    hot_target = lax.broadcasted_iota(jnp.int32, (members, total), 0) == target
    hot_pair = lax.broadcasted_iota(jnp.int32, (members * members, total), 0) == pair
    return lax.dot_general(
        jnp.where(hot_target, 1.0, 0.0).astype(jnp.bfloat16),
        jnp.where(hot_pair, 1.0, 0.0).astype(jnp.bfloat16),
        (((1,), (1,)), ((), ())),
        preferred_element_type=jnp.float32,
    )


def cycle_kernel(
    groups, members,
    amp, integ, tasks, counts, owner, out,
    swap, halves, mixed_t, got_t, weighed, parts, landed, table, numbers,
    swap_ss, swap_rs, int_ss, int_rs, mix_ss, mix_rs, part_ss, part_rs, table_sem,
):
    grp, mem = lax.axis_index("grp"), lax.axis_index("mem")
    tile = amp.shape[-1]
    half, block, rounds = tile // 2, tile // groups, tile // STEP
    quarter = members // 2
    first_worker = members // 2 - 2
    workers = range(first_worker, first_worker + 4)
    plane, side = lax.div(mem, 2), lax.rem(mem, 2)
    area = lax.div(mem, quarter)
    works = (mem >= first_worker) & (mem < first_worker + 4)
    own_rows = pl.ds(pl.multiple_of(side * half, half), half)

    barrier = pltpu.get_barrier_semaphore()
    for turn in range(1, groups):
        pl.semaphore_signal(
            barrier, inc=1, device_id={"grp": lax.rem(grp + turn, groups)}, device_id_type=MESH
        )
    for turn in range(1, members):
        pl.semaphore_signal(
            barrier, inc=1, device_id={"mem": lax.rem(mem + turn, members)}, device_id_type=MESH
        )
    pl.semaphore_wait(barrier, groups + members - 2)

    def swap_copy(peer):
        return remote(
            amp.at[0, 0, pl.ds(pl.multiple_of(peer * block, block), block)],
            swap.at[grp], swap_ss.at[peer], swap_rs.at[grp], grp=peer,
        )

    def int_copy(index, worker):
        return remote(
            integ.at[0, 0, pl.ds((worker % 2) * half, half)],
            halves.at[mem], int_ss.at[index], int_rs.at[mem], mem=worker,
        )

    def mix_copy(turn, index, worker):
        return remote(
            mixed_t.at[turn, pl.ds((worker % 2) * half, half)],
            got_t.at[turn, mem], mix_ss.at[turn, index], mix_rs.at[turn, mem], mem=worker,
        )

    def part_copy(turn, index, target):
        rows = pl.ds(turn * STEP, STEP)
        return remote(
            parts.at[index, rows], landed.at[side, rows],
            part_ss.at[turn, index], part_rs.at[turn, side], mem=target,
        )

    for turn in range(1, groups):
        swap_copy(lax.rem(grp + turn, groups)).start()
    for index, worker in enumerate(workers):
        @pl.when(mem != worker)
        def _():
            int_copy(index, worker).start()

    own_block = pl.ds(pl.multiple_of(grp * block, block), block)
    swap[grp] = amp[0, 0, own_block]

    @pl.when(works)
    def _():
        halves[mem] = integ[0, 0, own_rows]
        table[...] = count_tasks(members, tasks, counts, owner)
        to_scalar = pltpu.make_async_copy(table, numbers, table_sem)
        to_scalar.start()
        to_scalar.wait()

    for turn in range(1, groups):
        peer = lax.rem(grp + turn, groups)
        remote(
            swap.at[peer], swap.at[peer], swap_ss.at[peer], swap_rs.at[peer], grp=peer
        ).wait_recv()
    for turn in range(rounds):
        rows = pl.ds(turn * STEP, STEP)
        swapped = swap[...].reshape(tile, tile)[turn * STEP : (turn + 1) * STEP]
        mixed = (
            2.0 * amp[0, 0, rows].astype(jnp.float32) - swapped.astype(jnp.float32)
        )
        mixed_t[turn] = mixed.T.astype(jnp.bfloat16)
        for index, worker in enumerate(workers):
            @pl.when(mem != worker)
            def _():
                mix_copy(turn, index, worker).start()

        @pl.when(works)
        def _():
            got_t[turn, mem] = mixed_t[turn, own_rows]

    @pl.when(works)
    def _():
        for source in range(members):
            @pl.when(mem != source)
            def _():
                remote(
                    halves.at[source], halves.at[source],
                    int_ss.at[0], int_rs.at[source], mem=source,
                ).wait_recv()

        def weigh(index, carry):
            rows = pl.ds(pl.multiple_of(index * 16, 16), 16)
            read = [halves[b, rows].astype(jnp.float32) for b in range(members)]
            for a in range(members):
                for q in range(quarter):
                    total = jnp.zeros((16, tile), jnp.float32)
                    for b in range(members):
                        total += numbers[area * quarter + q, a * members + b] * read[b]
                    weighed[q, a, rows] = total.astype(jnp.bfloat16)
            return carry

        lax.fori_loop(0, half // 16, weigh, 0)

        for turn in range(rounds):
            rows = pl.ds(turn * STEP, STEP)
            for source in range(members):
                @pl.when(mem != source)
                def _():
                    remote(
                        got_t.at[turn, source], got_t.at[turn, source],
                        mix_ss.at[turn, 0], mix_rs.at[turn, source], mem=source,
                    ).wait_recv()
            left = got_t[turn].reshape(members * half, STEP).T
            for q in range(quarter):
                target = area * quarter + q
                parts[q, rows] = jnp.dot(
                    left, weighed[q].reshape(members * half, tile),
                    preferred_element_type=jnp.float32,
                ).astype(jnp.bfloat16)

                @pl.when(mem != target)
                def _():
                    part_copy(turn, q, target).start()

                @pl.when(mem == target)
                def _():
                    landed[side, rows] = parts[q, rows]

    for turn in range(rounds):
        rows = pl.ds(turn * STEP, STEP)
        for sender_side in range(2):
            sender = lax.min(lax.max(plane, quarter // 2 - 1), quarter // 2) * 2 + sender_side

            @pl.when(mem != sender)
            def _():
                remote(
                    landed.at[sender_side, rows], landed.at[sender_side, rows],
                    part_ss.at[turn, 0], part_rs.at[turn, sender_side], mem=sender,
                ).wait_recv()
        out[0, 0, rows] = (
            landed[0, rows].astype(jnp.float32) + landed[1, rows].astype(jnp.float32)
        ).astype(jnp.bfloat16)

    for turn in range(1, groups):
        swap_copy(lax.rem(grp + turn, groups)).wait_send()
    for index, worker in enumerate(workers):
        @pl.when(mem != worker)
        def _():
            int_copy(index, worker).wait_send()
            for turn in range(rounds):
                mix_copy(turn, index, worker).wait_send()

    @pl.when(works)
    def _():
        for q in range(quarter):
            target = area * quarter + q

            @pl.when(mem != target)
            def _():
                for turn in range(rounds):
                    part_copy(turn, q, target).wait_send()


def local_workers(amplitudes, integrals, task_list, task_counts, owner_map):
    groups, members = lax.axis_size("grp"), lax.axis_size("mem")
    tile = amplitudes.shape[-1]
    half, rounds, quarter = tile // 2, tile // STEP, members // 2
    vmem = pl.BlockSpec(memory_space=pltpu.VMEM)
    smem = pl.BlockSpec(memory_space=pltpu.SMEM)
    dma = pltpu.SemaphoreType.DMA
    bf16 = jnp.bfloat16
    return pl.pallas_call(
        functools.partial(cycle_kernel, groups, members),
        out_shape=jax.ShapeDtypeStruct(amplitudes.shape, bf16),
        in_specs=[vmem, vmem, vmem, smem, smem],
        out_specs=vmem,
        scratch_shapes=[
            pltpu.VMEM((groups, tile // groups, tile), bf16),
            pltpu.VMEM((members, half, tile), bf16),
            pltpu.VMEM((rounds, tile, STEP), bf16),
            pltpu.VMEM((rounds, members, half, STEP), bf16),
            pltpu.VMEM((quarter, members, half, tile), bf16),
            pltpu.VMEM((quarter, tile, tile), bf16),
            pltpu.VMEM((2, tile, tile), bf16),
            pltpu.VMEM((members, members * members), jnp.float32),
            pltpu.SMEM((members, members * members), jnp.float32),
            dma((groups,)), dma((groups,)),
            dma((4,)), dma((members,)),
            dma((rounds, 4)), dma((rounds, members)),
            dma((rounds, quarter)), dma((rounds, 2)),
            dma,
        ],
        compiler_params=pltpu.CompilerParams(
            collective_id=0, has_side_effects=True, vmem_limit_bytes=40 * 1024 * 1024
        ),
    )(amplitudes, integrals, jnp.transpose(task_list, (2, 0, 1)), task_counts, owner_map)


def solution(mesh):
    placed = (
        P("grp", "mem", None, None),
        P("grp", "mem", None, None),
        P("grp", None, None),
        P("grp", None),
        P(),
    )
    body = local_workers if mesh.shape["mem"] == 2 * 4 else local
    return jax.shard_map(
        body, mesh=mesh, in_specs=placed, out_specs=P("grp", "mem", None, None), check_vma=False
    )
```

```python
import functools
import math

import jax
import jax.numpy as jnp
from jax import lax
from jax.experimental import pallas as pl
from jax.experimental.pallas import tpu as pltpu
from jax.sharding import PartitionSpec as P

TASK_DEV = 64


def block_products(got_mixed, got_int, picked, living):
    left_tile = jnp.take(got_mixed, picked[:, 1], axis=0)
    right_tile = jnp.take(got_int, picked[:, 2], axis=0)
    product = jnp.einsum("kxy,kyz->kxz", left_tile, right_tile, preferred_element_type=jnp.float32)
    return jnp.where(living[:, None, None], product, jnp.float32(0.0))


def add_targets(running, targets, living, product):
    safe_targets = jnp.where(living, targets, 0)
    return running.at[safe_targets].add(product)


def local(amplitudes, integrals, task_list, task_counts, owner_map):
    tile_order = amplitudes.shape[-1]
    members = lax.axis_size("mem")
    device = lax.axis_index("mem")
    slot_count = TASK_DEV
    own_amp = amplitudes[0, 0]
    swapped = lax.all_to_all(own_amp, "grp", split_axis=0, concat_axis=0, tiled=True)
    mixed_tile = (2.0 * own_amp.astype(jnp.float32) - swapped.astype(jnp.float32)).astype(
        jnp.bfloat16
    )
    own_int = integrals[0, 0]
    holders = jnp.take(owner_map, task_list[0], axis=0)
    live_all = jnp.arange(slot_count, dtype=jnp.int32)[None, :] < task_counts[0][:, None]
    got_mixed, got_int = (
        lax.all_gather(mixed_tile[None], "mem", axis=0, tiled=True),
        lax.all_gather(own_int[None], "mem", axis=0, tiled=True),
    )
    flat_live = live_all.reshape(-1)
    mine = flat_live & (holders[:, 0] == device)
    order = jnp.argsort(jnp.where(mine, 0, 1).astype(jnp.int32), stable=True)
    total_mine = jnp.sum(mine.astype(jnp.int32))
    block_size = math.gcd(members * slot_count, 16)
    block_count = (total_mine + block_size - 1) // block_size
    slot_index = jnp.arange(block_size, dtype=jnp.int32)

    def owner_step(state):
        turn, per_exec = state
        first = turn * block_size
        chosen = lax.dynamic_slice_in_dim(order, first, block_size, 0)
        picked = jnp.take(holders, chosen, axis=0)
        living = slot_index + first < total_mine
        product = block_products(got_mixed, got_int, picked, living)
        return (turn + 1, add_targets(per_exec, chosen // slot_count, living, product))

    start_exec = jnp.zeros((members, tile_order, tile_order), jnp.float32)
    _, per_exec = lax.while_loop(
        lambda state: state[0] < block_count, owner_step, (jnp.int32(0), start_exec)
    )
    summed = jnp.sum(per_exec.astype(jnp.bfloat16), axis=0, dtype=jnp.float32)
    return summed.astype(jnp.bfloat16)[None, None]


MESH = pl.DeviceIdType.MESH
STEP = 128
BAND = 32
VMEM_BYTES = 65280 * 1024


def remote(src, dst, send_sem, recv_sem, **place):
    return pltpu.make_async_remote_copy(
        src_ref=src, dst_ref=dst, send_sem=send_sem, recv_sem=recv_sem,
        device_id=place, device_id_type=MESH,
    )


def spread_counts(members, quarter, area, tasks, counts, owner):
    total = tasks.shape[-1]
    slots = total // members
    ids = [tasks[field] for field in range(3)]
    rows = [jnp.zeros((1, total), jnp.int32) for _ in range(3)]
    for tile_id in range(members):
        row = owner[tile_id]
        rows = [jnp.where(ids[f] == tile_id, row, rows[f]) for f in range(3)]
    place = lax.broadcasted_iota(jnp.int32, (1, total), 1)
    live = jnp.zeros((1, total), jnp.int32)
    for executor in range(members):
        offset = place - executor * slots
        inside = (offset >= 0) & (offset < jnp.minimum(counts[0, executor], slots))
        live = jnp.where(inside, 1, live)
    key = (rows[0] - area * quarter) * members + rows[1]
    key = jnp.where(live == 1, key, -1)
    tall, wide = quarter * members * BAND, members * BAND
    hot_left = lax.broadcasted_iota(jnp.int32, (tall, total), 0) // BAND == key
    hot_right = lax.broadcasted_iota(jnp.int32, (wide, total), 0) // BAND == rows[2]
    spread = lax.dot_general(
        jnp.where(hot_left, 1.0, 0.0).astype(jnp.bfloat16),
        jnp.where(hot_right, 1.0, 0.0).astype(jnp.bfloat16),
        (((1,), (1,)), ((), ())),
        preferred_element_type=jnp.float32,
    )
    down = lax.broadcasted_iota(jnp.int32, (tall, wide), 0) % BAND
    across = lax.broadcasted_iota(jnp.int32, (tall, wide), 1) % BAND
    return jnp.where(down == across, spread, 0.0).astype(jnp.bfloat16)


def cycle_kernel(
    groups, members,
    amp_hbm, integ, tasks_hbm, counts_hbm, owner_hbm, out,
    amp, tasks, counts, owner, result,
    swap, halves, mixed_t, got_t, weighed, parts, landed, spread,
    swap_ss, swap_rs, int_ss, int_rs, mix_ss, mix_rs, part_ss, part_rs, local_sem, out_sem,
):
    grp, mem = lax.axis_index("grp"), lax.axis_index("mem")
    tile = amp.shape[-1]
    half, block, rounds = tile // 2, tile // groups, tile // STEP
    quarter = members // 2
    first_worker = members // 2 - 2
    workers = range(first_worker, first_worker + 4)
    plane, side = lax.div(mem, 2), lax.rem(mem, 2)
    area = lax.div(mem, quarter)
    works = (mem >= first_worker) & (mem < first_worker + 4)
    own_rows = pl.ds(pl.multiple_of(side * half, half), half)

    amp_in = pltpu.make_async_copy(amp_hbm, amp, local_sem.at[0])
    tasks_in = pltpu.make_async_copy(tasks_hbm, tasks, local_sem.at[1])
    counts_in = pltpu.make_async_copy(counts_hbm, counts, local_sem.at[2])
    owner_in = pltpu.make_async_copy(owner_hbm, owner, local_sem.at[3])
    half_in = pltpu.make_async_copy(integ.at[0, 0, own_rows], halves.at[mem], local_sem.at[4])
    amp_in.start()

    @pl.when(works)
    def _():
        tasks_in.start()
        counts_in.start()
        owner_in.start()
        half_in.start()

    barrier = pltpu.get_barrier_semaphore()
    for turn in range(1, groups):
        pl.semaphore_signal(
            barrier, inc=1, device_id={"grp": lax.rem(grp + turn, groups)}, device_id_type=MESH
        )
    for turn in range(1, members):
        pl.semaphore_signal(
            barrier, inc=1, device_id={"mem": lax.rem(mem + turn, members)}, device_id_type=MESH
        )
    pl.semaphore_wait(barrier, groups + members - 2)

    def swap_copy(peer):
        return remote(
            amp_hbm.at[0, 0, pl.ds(pl.multiple_of(peer * block, block), block)],
            swap.at[grp], swap_ss.at[peer], swap_rs.at[grp], grp=peer,
        )

    def int_copy(index, worker):
        return remote(
            integ.at[0, 0, pl.ds((worker % 2) * half, half)],
            halves.at[mem], int_ss.at[index], int_rs.at[mem], mem=worker,
        )

    def mix_copy(turn, index, worker):
        return remote(
            mixed_t.at[turn, pl.ds((worker % 2) * half, half)],
            got_t.at[turn, mem], mix_ss.at[turn, index], mix_rs.at[turn, mem], mem=worker,
        )

    def part_copy(turn, index, target):
        rows = pl.ds(turn * STEP, STEP)
        return remote(
            parts.at[index, rows], landed.at[side, rows],
            part_ss.at[turn, index], part_rs.at[turn, side], mem=target,
        )

    def result_copy(turn):
        rows = pl.ds(turn * STEP, STEP)
        return pltpu.make_async_copy(result.at[rows], out.at[0, 0, rows], out_sem.at[turn])

    for turn in range(1, groups):
        swap_copy(lax.rem(grp + turn, groups)).start()
    for index, worker in enumerate(workers):
        @pl.when(mem != worker)
        def _():
            int_copy(index, worker).start()

    amp_in.wait()
    own_block = pl.ds(pl.multiple_of(grp * block, block), block)
    swap[grp] = amp[0, 0, own_block]

    @pl.when(works)
    def _():
        tasks_in.wait()
        counts_in.wait()
        owner_in.wait()
        half_in.wait()
        spread[...] = spread_counts(members, quarter, area, tasks, counts, owner)

    for turn in range(1, groups):
        peer = lax.rem(grp + turn, groups)
        remote(
            swap.at[peer], swap.at[peer], swap_ss.at[peer], swap_rs.at[peer], grp=peer
        ).wait_recv()
    for turn in range(rounds):
        rows = pl.ds(turn * STEP, STEP)
        swapped = swap[...].reshape(tile, tile)[turn * STEP : (turn + 1) * STEP]
        mixed = (
            2.0 * amp[0, 0, rows].astype(jnp.float32) - swapped.astype(jnp.float32)
        )
        mixed_t[turn] = mixed.T.astype(jnp.bfloat16)
        for index, worker in enumerate(workers):
            @pl.when(mem != worker)
            def _():
                mix_copy(turn, index, worker).start()

        @pl.when(works)
        def _():
            got_t[turn, mem] = mixed_t[turn, own_rows]

    @pl.when(works)
    def _():
        for source in range(members):
            @pl.when(mem != source)
            def _():
                remote(
                    halves.at[source], halves.at[source],
                    int_ss.at[0], int_rs.at[source], mem=source,
                ).wait_recv()

        def weigh(index, carry):
            rows = pl.ds(pl.multiple_of(index * BAND, BAND), BAND)
            sums = jnp.dot(
                spread[...], halves[:, rows].reshape(members * BAND, tile),
                preferred_element_type=jnp.float32,
            )
            weighed[:, :, rows] = sums.astype(jnp.bfloat16).reshape(quarter, members, BAND, tile)
            return carry

        lax.fori_loop(0, half // BAND, weigh, 0)

        for turn in range(rounds):
            rows = pl.ds(turn * STEP, STEP)
            for source in range(members):
                @pl.when(mem != source)
                def _():
                    remote(
                        got_t.at[turn, source], got_t.at[turn, source],
                        mix_ss.at[turn, 0], mix_rs.at[turn, source], mem=source,
                    ).wait_recv()
            left = got_t[turn].reshape(members * half, STEP).T
            for q in range(quarter):
                target = area * quarter + q
                parts[q, rows] = jnp.dot(
                    left, weighed[q].reshape(members * half, tile),
                    preferred_element_type=jnp.float32,
                ).astype(jnp.bfloat16)

                @pl.when(mem != target)
                def _():
                    part_copy(turn, q, target).start()

                @pl.when(mem == target)
                def _():
                    landed[side, rows] = parts[q, rows]

    for turn in range(rounds):
        rows = pl.ds(turn * STEP, STEP)
        for sender_side in range(2):
            sender = lax.min(lax.max(plane, quarter // 2 - 1), quarter // 2) * 2 + sender_side

            @pl.when(mem != sender)
            def _():
                remote(
                    landed.at[sender_side, rows], landed.at[sender_side, rows],
                    part_ss.at[turn, 0], part_rs.at[turn, sender_side], mem=sender,
                ).wait_recv()
        result[rows] = (
            landed[0, rows].astype(jnp.float32) + landed[1, rows].astype(jnp.float32)
        ).astype(jnp.bfloat16)
        result_copy(turn).start()

    for turn in range(1, groups):
        swap_copy(lax.rem(grp + turn, groups)).wait_send()
    for index, worker in enumerate(workers):
        @pl.when(mem != worker)
        def _():
            int_copy(index, worker).wait_send()
            for turn in range(rounds):
                mix_copy(turn, index, worker).wait_send()

    @pl.when(works)
    def _():
        for q in range(quarter):
            target = area * quarter + q

            @pl.when(mem != target)
            def _():
                for turn in range(rounds):
                    part_copy(turn, q, target).wait_send()

    for turn in range(rounds):
        result_copy(turn).wait()


def local_workers(amplitudes, integrals, task_list, task_counts, owner_map):
    groups, members = lax.axis_size("grp"), lax.axis_size("mem")
    tile = amplitudes.shape[-1]
    half, rounds, quarter = tile // 2, tile // STEP, members // 2
    hbm = pl.BlockSpec(memory_space=pltpu.HBM)
    dma = pltpu.SemaphoreType.DMA
    bf16 = jnp.bfloat16
    return pl.pallas_call(
        functools.partial(cycle_kernel, groups, members),
        out_shape=jax.ShapeDtypeStruct(amplitudes.shape, bf16),
        in_specs=[hbm] * 5,
        out_specs=hbm,
        scratch_shapes=[
            pltpu.VMEM(amplitudes.shape, bf16),
            pltpu.VMEM((3, 1, task_list.shape[1]), jnp.int32),
            pltpu.SMEM(task_counts.shape, jnp.int32),
            pltpu.SMEM(owner_map.shape, jnp.int32),
            pltpu.VMEM((tile, tile), bf16),
            pltpu.VMEM((groups, tile // groups, tile), bf16),
            pltpu.VMEM((members, half, tile), bf16),
            pltpu.VMEM((rounds, tile, STEP), bf16),
            pltpu.VMEM((rounds, members, half, STEP), bf16),
            pltpu.VMEM((quarter, members, half, tile), bf16),
            pltpu.VMEM((quarter, tile, tile), bf16),
            pltpu.VMEM((2, tile, tile), bf16),
            pltpu.VMEM((quarter * members * BAND, members * BAND), bf16),
            dma((groups,)), dma((groups,)),
            dma((4,)), dma((members,)),
            dma((rounds, 4)), dma((rounds, members)),
            dma((rounds, quarter)), dma((rounds, 2)),
            dma((5,)), dma((rounds,)),
        ],
        compiler_params=pltpu.CompilerParams(
            collective_id=0, has_side_effects=True, vmem_limit_bytes=VMEM_BYTES
        ),
    )(amplitudes, integrals, jnp.transpose(task_list, (2, 0, 1)), task_counts, owner_map)


def solution(mesh):
    placed = (
        P("grp", "mem", None, None),
        P("grp", "mem", None, None),
        P("grp", None, None),
        P("grp", None),
        P(),
    )
    body = local_workers if mesh.shape["mem"] == 2 * 4 else local
    return jax.shard_map(
        body, mesh=mesh, in_specs=placed, out_specs=P("grp", "mem", None, None), check_vma=False
    )
```

```python
import functools
import math

import jax
import jax.numpy as jnp
from jax import lax
from jax.experimental import pallas as pl
from jax.experimental.pallas import tpu as pltpu
from jax.sharding import PartitionSpec as P

TASK_DEV = 64


def block_products(got_mixed, got_int, picked, living):
    left_tile = jnp.take(got_mixed, picked[:, 1], axis=0)
    right_tile = jnp.take(got_int, picked[:, 2], axis=0)
    product = jnp.einsum("kxy,kyz->kxz", left_tile, right_tile, preferred_element_type=jnp.float32)
    return jnp.where(living[:, None, None], product, jnp.float32(0.0))


def add_targets(running, targets, living, product):
    safe_targets = jnp.where(living, targets, 0)
    return running.at[safe_targets].add(product)


def local(amplitudes, integrals, task_list, task_counts, owner_map):
    tile_order = amplitudes.shape[-1]
    members = lax.axis_size("mem")
    device = lax.axis_index("mem")
    slot_count = TASK_DEV
    own_amp = amplitudes[0, 0]
    swapped = lax.all_to_all(own_amp, "grp", split_axis=0, concat_axis=0, tiled=True)
    mixed_tile = (2.0 * own_amp.astype(jnp.float32) - swapped.astype(jnp.float32)).astype(
        jnp.bfloat16
    )
    own_int = integrals[0, 0]
    holders = jnp.take(owner_map, task_list[0], axis=0)
    live_all = jnp.arange(slot_count, dtype=jnp.int32)[None, :] < task_counts[0][:, None]
    got_mixed, got_int = (
        lax.all_gather(mixed_tile[None], "mem", axis=0, tiled=True),
        lax.all_gather(own_int[None], "mem", axis=0, tiled=True),
    )
    flat_live = live_all.reshape(-1)
    mine = flat_live & (holders[:, 0] == device)
    order = jnp.argsort(jnp.where(mine, 0, 1).astype(jnp.int32), stable=True)
    total_mine = jnp.sum(mine.astype(jnp.int32))
    block_size = math.gcd(members * slot_count, 16)
    block_count = (total_mine + block_size - 1) // block_size
    slot_index = jnp.arange(block_size, dtype=jnp.int32)

    def owner_step(state):
        turn, per_exec = state
        first = turn * block_size
        chosen = lax.dynamic_slice_in_dim(order, first, block_size, 0)
        picked = jnp.take(holders, chosen, axis=0)
        living = slot_index + first < total_mine
        product = block_products(got_mixed, got_int, picked, living)
        return (turn + 1, add_targets(per_exec, chosen // slot_count, living, product))

    start_exec = jnp.zeros((members, tile_order, tile_order), jnp.float32)
    _, per_exec = lax.while_loop(
        lambda state: state[0] < block_count, owner_step, (jnp.int32(0), start_exec)
    )
    summed = jnp.sum(per_exec.astype(jnp.bfloat16), axis=0, dtype=jnp.float32)
    return summed.astype(jnp.bfloat16)[None, None]


MESH = pl.DeviceIdType.MESH
STEP = 128
BAND = 32
VMEM_BYTES = 65280 * 1024


def remote(src, dst, send_sem, recv_sem, **place):
    return pltpu.make_async_remote_copy(
        src_ref=src, dst_ref=dst, send_sem=send_sem, recv_sem=recv_sem,
        device_id=place, device_id_type=MESH,
    )


def spread_counts(members, quarter, area, tasks, counts, owner):
    total = tasks.shape[-1]
    slots = total // members
    ids = [tasks[field] for field in range(3)]
    rows = [jnp.zeros((1, total), jnp.int32) for _ in range(3)]
    for tile_id in range(members):
        row = owner[tile_id]
        rows = [jnp.where(ids[f] == tile_id, row, rows[f]) for f in range(3)]
    place = lax.broadcasted_iota(jnp.int32, (1, total), 1)
    live = jnp.zeros((1, total), jnp.int32)
    for executor in range(members):
        offset = place - executor * slots
        inside = (offset >= 0) & (offset < jnp.minimum(counts[0, executor], slots))
        live = jnp.where(inside, 1, live)
    key = (rows[0] - area * quarter) * members + rows[1]
    key = jnp.where(live == 1, key, -1)
    tall, wide = quarter * members * BAND, members * BAND
    hot_left = lax.broadcasted_iota(jnp.int32, (tall, total), 0) // BAND == key
    hot_right = lax.broadcasted_iota(jnp.int32, (wide, total), 0) // BAND == rows[2]
    spread = lax.dot_general(
        jnp.where(hot_left, 1.0, 0.0).astype(jnp.bfloat16),
        jnp.where(hot_right, 1.0, 0.0).astype(jnp.bfloat16),
        (((1,), (1,)), ((), ())),
        preferred_element_type=jnp.float32,
    )
    down = lax.broadcasted_iota(jnp.int32, (tall, wide), 0) % BAND
    across = lax.broadcasted_iota(jnp.int32, (tall, wide), 1) % BAND
    return jnp.where(down == across, spread, 0.0).astype(jnp.bfloat16)


def cycle_kernel(
    groups, members,
    amp_hbm, integ, tasks_hbm, counts_hbm, owner_hbm, out,
    amp, tasks, counts, owner, result,
    swap, halves, mixed_t, got_t, weighed, parts, landed, spread,
    swap_ss, swap_rs, int_ss, int_rs, mix_ss, mix_rs, part_ss, part_rs, local_sem, out_sem,
):
    grp, mem = lax.axis_index("grp"), lax.axis_index("mem")
    tile = amp.shape[-1]
    half, block, rounds = tile // 2, tile // groups, tile // STEP
    quarter = members // 2
    first_worker = members // 2 - 2
    plane, side = lax.div(mem, 2), lax.rem(mem, 2)
    area = lax.div(mem, quarter)
    works = (mem >= first_worker) & (mem < first_worker + 4)
    own_rows = pl.ds(pl.multiple_of(side * half, half), half)

    amp_in = pltpu.make_async_copy(amp_hbm, amp, local_sem.at[0])
    tasks_in = pltpu.make_async_copy(tasks_hbm, tasks, local_sem.at[1])
    counts_in = pltpu.make_async_copy(counts_hbm, counts, local_sem.at[2])
    owner_in = pltpu.make_async_copy(owner_hbm, owner, local_sem.at[3])
    half_in = pltpu.make_async_copy(integ.at[0, 0, own_rows], halves.at[mem], local_sem.at[4])
    amp_in.start()

    @pl.when(works)
    def _():
        tasks_in.start()
        counts_in.start()
        owner_in.start()
        half_in.start()

    barrier = pltpu.get_barrier_semaphore()
    for turn in range(1, groups):
        pl.semaphore_signal(
            barrier, inc=1, device_id={"grp": lax.rem(grp + turn, groups)}, device_id_type=MESH
        )
    for turn in range(1, members):
        pl.semaphore_signal(
            barrier, inc=1, device_id={"mem": lax.rem(mem + turn, members)}, device_id_type=MESH
        )
    pl.semaphore_wait(barrier, groups + members - 2)

    def swap_copy(peer):
        return remote(
            amp_hbm.at[0, 0, pl.ds(pl.multiple_of(peer * block, block), block)],
            swap.at[grp], swap_ss.at[peer], swap_rs.at[grp], grp=peer,
        )

    partner = mem + 1 - 2 * side
    other_rows = pl.ds(pl.multiple_of((1 - side) * half, half), half)
    lines = [(first_worker // 2 + index) * 2 + side for index in range(2)]

    def int_copy(index):
        if index == 0:
            source, slot, target = integ.at[0, 0, other_rows], mem, partner
        elif index < 3:
            source, slot, target = integ.at[0, 0, own_rows], mem, lines[index - 1]
        else:
            source, slot, target = halves.at[partner], partner, lines[index - 3]
        return remote(source, halves.at[slot], int_ss.at[index], int_rs.at[slot], mem=target)

    def mix_copy(turn, index):
        if index == 0:
            source, slot, target = mixed_t.at[turn, other_rows], mem, partner
        elif index < 3:
            source, slot, target = mixed_t.at[turn, own_rows], mem, lines[index - 1]
        else:
            source, slot, target = got_t.at[turn, partner], partner, lines[index - 3]
        return remote(
            source, got_t.at[turn, slot], mix_ss.at[turn, index], mix_rs.at[turn, slot], mem=target
        )

    def int_arrival(source):
        return remote(
            halves.at[source], halves.at[source], int_ss.at[0], int_rs.at[source], mem=partner
        )

    def mix_arrival(turn, source):
        return remote(
            got_t.at[turn, source], got_t.at[turn, source],
            mix_ss.at[turn, 0], mix_rs.at[turn, source], mem=partner,
        )

    def along_lines(first, do):
        for index in range(2):
            @pl.when(mem != lines[index])
            def _():
                do(first + index)

    def part_copy(turn, index, target):
        rows = pl.ds(turn * STEP, STEP)
        return remote(
            parts.at[index, rows], landed.at[side, rows],
            part_ss.at[turn, index], part_rs.at[turn, side], mem=target,
        )

    def result_copy(turn):
        rows = pl.ds(turn * STEP, STEP)
        return pltpu.make_async_copy(result.at[rows], out.at[0, 0, rows], out_sem.at[turn])

    for turn in range(1, groups):
        swap_copy(lax.rem(grp + turn, groups)).start()
    int_copy(0).start()
    along_lines(1, lambda index: int_copy(index).start())

    amp_in.wait()
    own_block = pl.ds(pl.multiple_of(grp * block, block), block)
    swap[grp] = amp[0, 0, own_block]

    @pl.when(works)
    def _():
        tasks_in.wait()
        counts_in.wait()
        owner_in.wait()
        half_in.wait()
        spread[...] = spread_counts(members, quarter, area, tasks, counts, owner)

    int_arrival(partner).wait_recv()
    along_lines(3, lambda index: int_copy(index).start())
    for turn in range(1, groups):
        peer = lax.rem(grp + turn, groups)
        remote(
            swap.at[peer], swap.at[peer], swap_ss.at[peer], swap_rs.at[peer], grp=peer
        ).wait_recv()
    for turn in range(rounds):
        rows = pl.ds(turn * STEP, STEP)
        swapped = swap[...].reshape(tile, tile)[turn * STEP : (turn + 1) * STEP]
        mixed = (
            2.0 * amp[0, 0, rows].astype(jnp.float32) - swapped.astype(jnp.float32)
        )
        mixed_t[turn] = mixed.T.astype(jnp.bfloat16)
        mix_copy(turn, 0).start()
        along_lines(1, lambda index: mix_copy(turn, index).start())

        @pl.when(works)
        def _():
            got_t[turn, mem] = mixed_t[turn, own_rows]

    for turn in range(rounds):
        mix_arrival(turn, partner).wait_recv()
        along_lines(3, lambda index: mix_copy(turn, index).start())

    @pl.when(works)
    def _():
        for source in range(members):
            @pl.when(plane != source // 2)
            def _():
                int_arrival(source).wait_recv()

        def weigh(index, carry):
            rows = pl.ds(pl.multiple_of(index * BAND, BAND), BAND)
            sums = jnp.dot(
                spread[...], halves[:, rows].reshape(members * BAND, tile),
                preferred_element_type=jnp.float32,
            )
            weighed[:, :, rows] = sums.astype(jnp.bfloat16).reshape(quarter, members, BAND, tile)
            return carry

        lax.fori_loop(0, half // BAND, weigh, 0)

        for turn in range(rounds):
            rows = pl.ds(turn * STEP, STEP)
            for source in range(members):
                @pl.when(plane != source // 2)
                def _():
                    mix_arrival(turn, source).wait_recv()
            left = got_t[turn].reshape(members * half, STEP).T
            for q in range(quarter):
                target = area * quarter + q
                parts[q, rows] = jnp.dot(
                    left, weighed[q].reshape(members * half, tile),
                    preferred_element_type=jnp.float32,
                ).astype(jnp.bfloat16)

                @pl.when(mem != target)
                def _():
                    part_copy(turn, q, target).start()

                @pl.when(mem == target)
                def _():
                    landed[side, rows] = parts[q, rows]

    for turn in range(rounds):
        rows = pl.ds(turn * STEP, STEP)
        for sender_side in range(2):
            sender = lax.min(lax.max(plane, quarter // 2 - 1), quarter // 2) * 2 + sender_side

            @pl.when(mem != sender)
            def _():
                remote(
                    landed.at[sender_side, rows], landed.at[sender_side, rows],
                    part_ss.at[turn, 0], part_rs.at[turn, sender_side], mem=sender,
                ).wait_recv()
        result[rows] = (
            landed[0, rows].astype(jnp.float32) + landed[1, rows].astype(jnp.float32)
        ).astype(jnp.bfloat16)
        result_copy(turn).start()

    for turn in range(1, groups):
        swap_copy(lax.rem(grp + turn, groups)).wait_send()
    int_copy(0).wait_send()
    along_lines(1, lambda index: int_copy(index).wait_send())
    along_lines(3, lambda index: int_copy(index).wait_send())
    for turn in range(rounds):
        mix_copy(turn, 0).wait_send()
        along_lines(1, lambda index: mix_copy(turn, index).wait_send())
        along_lines(3, lambda index: mix_copy(turn, index).wait_send())

    @pl.when(works)
    def _():
        for q in range(quarter):
            target = area * quarter + q

            @pl.when(mem != target)
            def _():
                for turn in range(rounds):
                    part_copy(turn, q, target).wait_send()

    for turn in range(rounds):
        result_copy(turn).wait()


def local_workers(amplitudes, integrals, task_list, task_counts, owner_map):
    groups, members = lax.axis_size("grp"), lax.axis_size("mem")
    tile = amplitudes.shape[-1]
    half, rounds, quarter = tile // 2, tile // STEP, members // 2
    hbm = pl.BlockSpec(memory_space=pltpu.HBM)
    dma = pltpu.SemaphoreType.DMA
    bf16 = jnp.bfloat16
    return pl.pallas_call(
        functools.partial(cycle_kernel, groups, members),
        out_shape=jax.ShapeDtypeStruct(amplitudes.shape, bf16),
        in_specs=[hbm] * 5,
        out_specs=hbm,
        scratch_shapes=[
            pltpu.VMEM(amplitudes.shape, bf16),
            pltpu.VMEM((3, 1, task_list.shape[1]), jnp.int32),
            pltpu.SMEM(task_counts.shape, jnp.int32),
            pltpu.SMEM(owner_map.shape, jnp.int32),
            pltpu.VMEM((tile, tile), bf16),
            pltpu.VMEM((groups, tile // groups, tile), bf16),
            pltpu.VMEM((members, half, tile), bf16),
            pltpu.VMEM((rounds, tile, STEP), bf16),
            pltpu.VMEM((rounds, members, half, STEP), bf16),
            pltpu.VMEM((quarter, members, half, tile), bf16),
            pltpu.VMEM((quarter, tile, tile), bf16),
            pltpu.VMEM((2, tile, tile), bf16),
            pltpu.VMEM((quarter * members * BAND, members * BAND), bf16),
            dma((groups,)), dma((groups,)),
            dma((5,)), dma((members,)),
            dma((rounds, 5)), dma((rounds, members)),
            dma((rounds, quarter)), dma((rounds, 2)),
            dma((5,)), dma((rounds,)),
        ],
        compiler_params=pltpu.CompilerParams(
            collective_id=0, has_side_effects=True, vmem_limit_bytes=VMEM_BYTES
        ),
    )(amplitudes, integrals, jnp.transpose(task_list, (2, 0, 1)), task_counts, owner_map)


def solution(mesh):
    placed = (
        P("grp", "mem", None, None),
        P("grp", "mem", None, None),
        P("grp", None, None),
        P("grp", None),
        P(),
    )
    body = local_workers if mesh.shape["mem"] == 2 * 4 else local
    return jax.shard_map(
        body, mesh=mesh, in_specs=placed, out_specs=P("grp", "mem", None, None), check_vma=False
    )
```

```python
import functools
import math

import jax
import jax.numpy as jnp
from jax import lax
from jax.experimental import pallas as pl
from jax.experimental.pallas import tpu as pltpu
from jax.sharding import PartitionSpec as P

TASK_DEV = 64


def block_products(got_mixed, got_int, picked, living):
    left_tile = jnp.take(got_mixed, picked[:, 1], axis=0)
    right_tile = jnp.take(got_int, picked[:, 2], axis=0)
    product = jnp.einsum("kxy,kyz->kxz", left_tile, right_tile, preferred_element_type=jnp.float32)
    return jnp.where(living[:, None, None], product, jnp.float32(0.0))


def add_targets(running, targets, living, product):
    safe_targets = jnp.where(living, targets, 0)
    return running.at[safe_targets].add(product)


def local(amplitudes, integrals, task_list, task_counts, owner_map):
    tile_order = amplitudes.shape[-1]
    members = lax.axis_size("mem")
    device = lax.axis_index("mem")
    slot_count = TASK_DEV
    own_amp = amplitudes[0, 0]
    swapped = lax.all_to_all(own_amp, "grp", split_axis=0, concat_axis=0, tiled=True)
    mixed_tile = (2.0 * own_amp.astype(jnp.float32) - swapped.astype(jnp.float32)).astype(
        jnp.bfloat16
    )
    own_int = integrals[0, 0]
    holders = jnp.take(owner_map, task_list[0], axis=0)
    live_all = jnp.arange(slot_count, dtype=jnp.int32)[None, :] < task_counts[0][:, None]
    got_mixed, got_int = (
        lax.all_gather(mixed_tile[None], "mem", axis=0, tiled=True),
        lax.all_gather(own_int[None], "mem", axis=0, tiled=True),
    )
    flat_live = live_all.reshape(-1)
    mine = flat_live & (holders[:, 0] == device)
    order = jnp.argsort(jnp.where(mine, 0, 1).astype(jnp.int32), stable=True)
    total_mine = jnp.sum(mine.astype(jnp.int32))
    block_size = math.gcd(members * slot_count, 16)
    block_count = (total_mine + block_size - 1) // block_size
    slot_index = jnp.arange(block_size, dtype=jnp.int32)

    def owner_step(state):
        turn, per_exec = state
        first = turn * block_size
        chosen = lax.dynamic_slice_in_dim(order, first, block_size, 0)
        picked = jnp.take(holders, chosen, axis=0)
        living = slot_index + first < total_mine
        product = block_products(got_mixed, got_int, picked, living)
        return (turn + 1, add_targets(per_exec, chosen // slot_count, living, product))

    start_exec = jnp.zeros((members, tile_order, tile_order), jnp.float32)
    _, per_exec = lax.while_loop(
        lambda state: state[0] < block_count, owner_step, (jnp.int32(0), start_exec)
    )
    summed = jnp.sum(per_exec.astype(jnp.bfloat16), axis=0, dtype=jnp.float32)
    return summed.astype(jnp.bfloat16)[None, None]


MESH = pl.DeviceIdType.MESH
STEP = 128
BAND = 32
VMEM_BYTES = 65280 * 1024


def remote(src, dst, send_sem, recv_sem, **place):
    return pltpu.make_async_remote_copy(
        src_ref=src, dst_ref=dst, send_sem=send_sem, recv_sem=recv_sem,
        device_id=place, device_id_type=MESH,
    )


def spread_counts(members, quarter, area, tasks, counts, owner):
    total = tasks.shape[-1]
    slots = total // members
    ids = [tasks[field] for field in range(3)]
    rows = [jnp.zeros((1, total), jnp.int32) for _ in range(3)]
    for tile_id in range(members):
        row = owner[tile_id]
        rows = [jnp.where(ids[f] == tile_id, row, rows[f]) for f in range(3)]
    place = lax.broadcasted_iota(jnp.int32, (1, total), 1)
    live = jnp.zeros((1, total), jnp.int32)
    for executor in range(members):
        offset = place - executor * slots
        inside = (offset >= 0) & (offset < jnp.minimum(counts[0, executor], slots))
        live = jnp.where(inside, 1, live)
    key = (rows[0] - area * quarter) * members + rows[1]
    key = jnp.where(live == 1, key, -1)
    tall, wide = quarter * members * BAND, members * BAND
    hot_left = lax.broadcasted_iota(jnp.int32, (tall, total), 0) // BAND == key
    hot_right = lax.broadcasted_iota(jnp.int32, (wide, total), 0) // BAND == rows[2]
    spread = lax.dot_general(
        jnp.where(hot_left, 1.0, 0.0).astype(jnp.bfloat16),
        jnp.where(hot_right, 1.0, 0.0).astype(jnp.bfloat16),
        (((1,), (1,)), ((), ())),
        preferred_element_type=jnp.float32,
    )
    down = lax.broadcasted_iota(jnp.int32, (tall, wide), 0) % BAND
    across = lax.broadcasted_iota(jnp.int32, (tall, wide), 1) % BAND
    return jnp.where(down == across, spread, 0.0).astype(jnp.bfloat16)


def cycle_kernel(
    groups, members,
    amp_hbm, integ, tasks_hbm, counts_hbm, owner_hbm, out,
    amp, tasks, counts, owner, result,
    swap, halves, mixed_t, got_t, weighed, parts, landed, spread,
    swap_ss, swap_rs, int_ss, int_rs, mix_ss, mix_rs, part_ss, part_rs, local_sem, out_sem,
):
    grp, mem = lax.axis_index("grp"), lax.axis_index("mem")
    tile = amp.shape[-1]
    half, block, rounds = tile // 2, tile // groups, tile // STEP
    quarter = members // 2
    first_worker = members // 2 - 2
    workers = range(first_worker, first_worker + 4)
    plane, side = lax.div(mem, 2), lax.rem(mem, 2)
    area = lax.div(mem, quarter)
    works = (mem >= first_worker) & (mem < first_worker + 4)
    own_rows = pl.ds(pl.multiple_of(side * half, half), half)

    amp_in = pltpu.make_async_copy(amp_hbm, amp, local_sem.at[0])
    tasks_in = pltpu.make_async_copy(tasks_hbm, tasks, local_sem.at[1])
    counts_in = pltpu.make_async_copy(counts_hbm, counts, local_sem.at[2])
    owner_in = pltpu.make_async_copy(owner_hbm, owner, local_sem.at[3])
    half_in = pltpu.make_async_copy(integ.at[0, 0, own_rows], halves.at[mem], local_sem.at[4])
    amp_in.start()

    @pl.when(works)
    def _():
        tasks_in.start()
        counts_in.start()
        owner_in.start()
        half_in.start()

    barrier = pltpu.get_barrier_semaphore()
    for turn in range(1, groups):
        pl.semaphore_signal(
            barrier, inc=1, device_id={"grp": lax.rem(grp + turn, groups)}, device_id_type=MESH
        )
    for turn in range(1, members):
        pl.semaphore_signal(
            barrier, inc=1, device_id={"mem": lax.rem(mem + turn, members)}, device_id_type=MESH
        )
    pl.semaphore_wait(barrier, groups + members - 2)

    def swap_copy(peer):
        return remote(
            amp_hbm.at[0, 0, pl.ds(pl.multiple_of(peer * block, block), block)],
            swap.at[grp], swap_ss.at[peer], swap_rs.at[grp], grp=peer,
        )

    def int_copy(index, worker):
        return remote(
            integ.at[0, 0, pl.ds((worker % 2) * half, half)],
            halves.at[mem], int_ss.at[index], int_rs.at[mem], mem=worker,
        )

    def mix_copy(turn, index, worker):
        return remote(
            mixed_t.at[turn, pl.ds((worker % 2) * half, half)],
            got_t.at[turn, mem], mix_ss.at[turn, index], mix_rs.at[turn, mem], mem=worker,
        )

    def part_copy(turn, index, target):
        rows = pl.ds(turn * STEP, STEP)
        return remote(
            parts.at[index, rows], landed.at[side, rows],
            part_ss.at[turn, index], part_rs.at[turn, side], mem=target,
        )

    def result_copy(turn):
        rows = pl.ds(turn * STEP, STEP)
        return pltpu.make_async_copy(result.at[rows], out.at[0, 0, rows], out_sem.at[turn])

    for turn in range(1, groups):
        swap_copy(lax.rem(grp + turn, groups)).start()
    for index, worker in enumerate(workers):
        @pl.when(mem != worker)
        def _():
            int_copy(index, worker).start()

    amp_in.wait()
    own_block = pl.ds(pl.multiple_of(grp * block, block), block)
    swap[grp] = amp[0, 0, own_block]

    @pl.when(works)
    def _():
        tasks_in.wait()
        counts_in.wait()
        owner_in.wait()
        half_in.wait()
        spread[...] = spread_counts(members, quarter, area, tasks, counts, owner)

    for turn in range(1, groups):
        peer = lax.rem(grp + turn, groups)
        remote(
            swap.at[peer], swap.at[peer], swap_ss.at[peer], swap_rs.at[peer], grp=peer
        ).wait_recv()
    for turn in range(rounds):
        rows = pl.ds(turn * STEP, STEP)
        swapped = swap[...].reshape(tile, tile)[turn * STEP : (turn + 1) * STEP]
        mixed = (
            2.0 * amp[0, 0, rows].astype(jnp.float32) - swapped.astype(jnp.float32)
        )
        mixed_t[turn] = mixed.T.astype(jnp.bfloat16)
        @pl.when(works)
        def _():
            got_t[turn, mem] = mixed_t[turn, own_rows]

    def send_mixed(turn):
        for index, worker in enumerate(workers):
            @pl.when(mem != worker)
            def _():
                (mix_copy(turn - 1, index, worker) if turn else int_copy(index, worker)).wait_send()
        for index, worker in enumerate(workers):
            @pl.when(mem != worker)
            def _():
                mix_copy(turn, index, worker).start()

    send_mixed(0)

    @pl.when(jnp.logical_not(works))
    def _():
        for turn in range(1, rounds):
            send_mixed(turn)

    @pl.when(works)
    def _():
        for source in range(members):
            @pl.when(mem != source)
            def _():
                remote(
                    halves.at[source], halves.at[source],
                    int_ss.at[0], int_rs.at[source], mem=source,
                ).wait_recv()

        def weigh(index, carry):
            rows = pl.ds(pl.multiple_of(index * BAND, BAND), BAND)
            sums = jnp.dot(
                spread[...], halves[:, rows].reshape(members * BAND, tile),
                preferred_element_type=jnp.float32,
            )
            weighed[:, :, rows] = sums.astype(jnp.bfloat16).reshape(quarter, members, BAND, tile)
            return carry

        lax.fori_loop(0, half // BAND, weigh, 0)

        for turn in range(rounds):
            rows = pl.ds(turn * STEP, STEP)
            if turn + 1 < rounds:
                send_mixed(turn + 1)
            for source in range(members):
                @pl.when(mem != source)
                def _():
                    remote(
                        got_t.at[turn, source], got_t.at[turn, source],
                        mix_ss.at[turn, 0], mix_rs.at[turn, source], mem=source,
                    ).wait_recv()
            left = got_t[turn].reshape(members * half, STEP).T
            for q in range(quarter):
                target = area * quarter + q
                parts[q, rows] = jnp.dot(
                    left, weighed[q].reshape(members * half, tile),
                    preferred_element_type=jnp.float32,
                ).astype(jnp.bfloat16)

                @pl.when(mem != target)
                def _():
                    part_copy(turn, q, target).start()

                @pl.when(mem == target)
                def _():
                    landed[side, rows] = parts[q, rows]

    for turn in range(rounds):
        rows = pl.ds(turn * STEP, STEP)
        for sender_side in range(2):
            sender = lax.min(lax.max(plane, quarter // 2 - 1), quarter // 2) * 2 + sender_side

            @pl.when(mem != sender)
            def _():
                remote(
                    landed.at[sender_side, rows], landed.at[sender_side, rows],
                    part_ss.at[turn, 0], part_rs.at[turn, sender_side], mem=sender,
                ).wait_recv()
        result[rows] = (
            landed[0, rows].astype(jnp.float32) + landed[1, rows].astype(jnp.float32)
        ).astype(jnp.bfloat16)
        result_copy(turn).start()

    for turn in range(1, groups):
        swap_copy(lax.rem(grp + turn, groups)).wait_send()
    for index, worker in enumerate(workers):
        @pl.when(mem != worker)
        def _():
            mix_copy(rounds - 1, index, worker).wait_send()

    @pl.when(works)
    def _():
        for q in range(quarter):
            target = area * quarter + q

            @pl.when(mem != target)
            def _():
                for turn in range(rounds):
                    part_copy(turn, q, target).wait_send()

    for turn in range(rounds):
        result_copy(turn).wait()


def local_workers(amplitudes, integrals, task_list, task_counts, owner_map):
    groups, members = lax.axis_size("grp"), lax.axis_size("mem")
    tile = amplitudes.shape[-1]
    half, rounds, quarter = tile // 2, tile // STEP, members // 2
    hbm = pl.BlockSpec(memory_space=pltpu.HBM)
    dma = pltpu.SemaphoreType.DMA
    bf16 = jnp.bfloat16
    return pl.pallas_call(
        functools.partial(cycle_kernel, groups, members),
        out_shape=jax.ShapeDtypeStruct(amplitudes.shape, bf16),
        in_specs=[hbm] * 5,
        out_specs=hbm,
        scratch_shapes=[
            pltpu.VMEM(amplitudes.shape, bf16),
            pltpu.VMEM((3, 1, task_list.shape[1]), jnp.int32),
            pltpu.SMEM(task_counts.shape, jnp.int32),
            pltpu.SMEM(owner_map.shape, jnp.int32),
            pltpu.VMEM((tile, tile), bf16),
            pltpu.VMEM((groups, tile // groups, tile), bf16),
            pltpu.VMEM((members, half, tile), bf16),
            pltpu.VMEM((rounds, tile, STEP), bf16),
            pltpu.VMEM((rounds, members, half, STEP), bf16),
            pltpu.VMEM((quarter, members, half, tile), bf16),
            pltpu.VMEM((quarter, tile, tile), bf16),
            pltpu.VMEM((2, tile, tile), bf16),
            pltpu.VMEM((quarter * members * BAND, members * BAND), bf16),
            dma((groups,)), dma((groups,)),
            dma((4,)), dma((members,)),
            dma((rounds, 4)), dma((rounds, members)),
            dma((rounds, quarter)), dma((rounds, 2)),
            dma((5,)), dma((rounds,)),
        ],
        compiler_params=pltpu.CompilerParams(
            collective_id=0, has_side_effects=True, vmem_limit_bytes=VMEM_BYTES
        ),
    )(amplitudes, integrals, jnp.transpose(task_list, (2, 0, 1)), task_counts, owner_map)


def solution(mesh):
    placed = (
        P("grp", "mem", None, None),
        P("grp", "mem", None, None),
        P("grp", None, None),
        P("grp", None),
        P(),
    )
    body = local_workers if mesh.shape["mem"] == 2 * 4 else local
    return jax.shard_map(
        body, mesh=mesh, in_specs=placed, out_specs=P("grp", "mem", None, None), check_vma=False
    )
```

```python
import functools
import math

import jax
import jax.numpy as jnp
from jax import lax
from jax.experimental import pallas as pl
from jax.experimental.pallas import tpu as pltpu
from jax.sharding import PartitionSpec as P

TASK_DEV = 64


def block_products(got_mixed, got_int, picked, living):
    left_tile = jnp.take(got_mixed, picked[:, 1], axis=0)
    right_tile = jnp.take(got_int, picked[:, 2], axis=0)
    product = jnp.einsum("kxy,kyz->kxz", left_tile, right_tile, preferred_element_type=jnp.float32)
    return jnp.where(living[:, None, None], product, jnp.float32(0.0))


def add_targets(running, targets, living, product):
    safe_targets = jnp.where(living, targets, 0)
    return running.at[safe_targets].add(product)


def local(amplitudes, integrals, task_list, task_counts, owner_map):
    tile_order = amplitudes.shape[-1]
    members = lax.axis_size("mem")
    device = lax.axis_index("mem")
    slot_count = TASK_DEV
    own_amp = amplitudes[0, 0]
    swapped = lax.all_to_all(own_amp, "grp", split_axis=0, concat_axis=0, tiled=True)
    mixed_tile = (2.0 * own_amp.astype(jnp.float32) - swapped.astype(jnp.float32)).astype(
        jnp.bfloat16
    )
    own_int = integrals[0, 0]
    holders = jnp.take(owner_map, task_list[0], axis=0)
    live_all = jnp.arange(slot_count, dtype=jnp.int32)[None, :] < task_counts[0][:, None]
    got_mixed, got_int = (
        lax.all_gather(mixed_tile[None], "mem", axis=0, tiled=True),
        lax.all_gather(own_int[None], "mem", axis=0, tiled=True),
    )
    flat_live = live_all.reshape(-1)
    mine = flat_live & (holders[:, 0] == device)
    order = jnp.argsort(jnp.where(mine, 0, 1).astype(jnp.int32), stable=True)
    total_mine = jnp.sum(mine.astype(jnp.int32))
    block_size = math.gcd(members * slot_count, 16)
    block_count = (total_mine + block_size - 1) // block_size
    slot_index = jnp.arange(block_size, dtype=jnp.int32)

    def owner_step(state):
        turn, per_exec = state
        first = turn * block_size
        chosen = lax.dynamic_slice_in_dim(order, first, block_size, 0)
        picked = jnp.take(holders, chosen, axis=0)
        living = slot_index + first < total_mine
        product = block_products(got_mixed, got_int, picked, living)
        return (turn + 1, add_targets(per_exec, chosen // slot_count, living, product))

    start_exec = jnp.zeros((members, tile_order, tile_order), jnp.float32)
    _, per_exec = lax.while_loop(
        lambda state: state[0] < block_count, owner_step, (jnp.int32(0), start_exec)
    )
    summed = jnp.sum(per_exec.astype(jnp.bfloat16), axis=0, dtype=jnp.float32)
    return summed.astype(jnp.bfloat16)[None, None]


MESH = pl.DeviceIdType.MESH
STEP = 128
BAND = 32
VMEM_BYTES = 65280 * 1024


def remote(src, dst, send_sem, recv_sem, **place):
    return pltpu.make_async_remote_copy(
        src_ref=src, dst_ref=dst, send_sem=send_sem, recv_sem=recv_sem,
        device_id=place, device_id_type=MESH,
    )


def spread_counts(members, tasks, counts, owner):
    total = tasks.shape[-1]
    slots = total // members
    ids = [tasks[field] for field in range(3)]
    rows = [jnp.zeros((1, total), jnp.int32) for _ in range(3)]
    for tile_id in range(members):
        row = owner[tile_id]
        rows = [jnp.where(ids[f] == tile_id, row, rows[f]) for f in range(3)]
    place = lax.broadcasted_iota(jnp.int32, (1, total), 1)
    live = jnp.zeros((1, total), jnp.int32)
    for executor in range(members):
        offset = place - executor * slots
        inside = (offset >= 0) & (offset < jnp.minimum(counts[0, executor], slots))
        live = jnp.where(inside, 1, live)
    key = rows[0] * members + rows[1]
    key = jnp.where(live == 1, key, -1)
    tall, wide = members * members * BAND, members * BAND
    hot_left = lax.broadcasted_iota(jnp.int32, (tall, total), 0) // BAND == key
    hot_right = lax.broadcasted_iota(jnp.int32, (wide, total), 0) // BAND == rows[2]
    spread = lax.dot_general(
        jnp.where(hot_left, 1.0, 0.0).astype(jnp.bfloat16),
        jnp.where(hot_right, 1.0, 0.0).astype(jnp.bfloat16),
        (((1,), (1,)), ((), ())),
        preferred_element_type=jnp.float32,
    )
    down = lax.broadcasted_iota(jnp.int32, (tall, wide), 0) % BAND
    across = lax.broadcasted_iota(jnp.int32, (tall, wide), 1) % BAND
    return jnp.where(down == across, spread, 0.0).astype(jnp.bfloat16)


def cycle_kernel(
    groups, members,
    amp_hbm, integ, tasks_hbm, counts_hbm, owner_hbm, out,
    amp, tasks, counts, owner,
    swap, halves, mixed_t, got_t, weighed, given, taken, kept, final, spread,
    swap_ss, swap_rs, int_ss, int_rs, mix_ss, mix_rs, part_ss, part_rs, out_ss, out_rs, local_sem,
):
    grp, mem = lax.axis_index("grp"), lax.axis_index("mem")
    tile = amp.shape[-1]
    half, block, rounds, planes = tile // 2, tile // groups, tile // STEP, members // 2
    plane, side = lax.div(mem, 2), lax.rem(mem, 2)
    partner = mem + 1 - 2 * side
    work_plane = planes // 2 - 1 + lax.rem(grp, 2)
    works = plane == work_plane
    own_rows = pl.ds(pl.multiple_of(side * half, half), half)

    amp_in = pltpu.make_async_copy(amp_hbm, amp, local_sem.at[0])
    tasks_in = pltpu.make_async_copy(tasks_hbm, tasks, local_sem.at[1])
    counts_in = pltpu.make_async_copy(counts_hbm, counts, local_sem.at[2])
    owner_in = pltpu.make_async_copy(owner_hbm, owner, local_sem.at[3])
    half_in = pltpu.make_async_copy(integ.at[0, 0, own_rows], halves.at[mem], local_sem.at[4])
    amp_in.start()

    @pl.when(works)
    def _():
        tasks_in.start()
        counts_in.start()
        owner_in.start()
        half_in.start()

    barrier = pltpu.get_barrier_semaphore()
    for turn in range(1, groups):
        pl.semaphore_signal(
            barrier, inc=1, device_id={"grp": lax.rem(grp + turn, groups)}, device_id_type=MESH
        )

    @pl.when(works)
    def _():
        for turn in range(1, members):
            pl.semaphore_signal(
                barrier, inc=1, device_id={"mem": lax.rem(mem + turn, members)}, device_id_type=MESH
            )
        pl.semaphore_wait(barrier, groups + members - 2)

    @pl.when(jnp.logical_not(works))
    def _():
        for worker_side in range(2):
            pl.semaphore_signal(
                barrier, inc=1, device_id={"mem": work_plane * 2 + worker_side}, device_id_type=MESH
            )
        pl.semaphore_wait(barrier, groups + 1)

    def swap_copy(peer):
        return remote(
            amp_hbm.at[0, 0, pl.ds(pl.multiple_of(peer * block, block), block)],
            swap.at[grp], swap_ss.at[peer], swap_rs.at[grp], grp=peer,
        )

    def int_copy(worker_side):
        return remote(
            integ.at[0, 0, pl.ds(worker_side * half, half)],
            halves.at[mem], int_ss.at[worker_side], int_rs.at[mem],
            mem=work_plane * 2 + worker_side,
        )

    def mix_copy(turn, worker_side):
        return remote(
            mixed_t.at[turn, pl.ds(worker_side * half, half)],
            got_t.at[turn, mem], mix_ss.at[turn, worker_side], mix_rs.at[turn, mem],
            mem=work_plane * 2 + worker_side,
        )

    def part_copy(turn, row):
        return remote(
            given.at[turn, row], taken.at[turn, row],
            part_ss.at[turn, row], part_rs.at[turn, row], mem=partner,
        )

    def out_copy(turn, row):
        return remote(
            final.at[turn, row], out.at[0, 0, pl.ds(turn * STEP, STEP)],
            out_ss.at[turn, row], out_rs.at[turn], mem=row * 2 + side,
        )

    def own_copy(turn):
        return pltpu.make_async_copy(
            final.at[turn, plane], out.at[0, 0, pl.ds(turn * STEP, STEP)], out_rs.at[turn]
        )

    def to_workers(do):
        for worker_side in range(2):
            @pl.when(mem != work_plane * 2 + worker_side)
            def _():
                do(worker_side)

    for turn in range(1, groups):
        swap_copy(lax.rem(grp + turn, groups)).start()
    to_workers(lambda worker_side: int_copy(worker_side).start())

    amp_in.wait()
    own_block = pl.ds(pl.multiple_of(grp * block, block), block)
    swap[grp] = amp[0, 0, own_block]

    for turn in range(1, groups):
        peer = lax.rem(grp + turn, groups)
        remote(
            swap.at[peer], swap.at[peer], swap_ss.at[peer], swap_rs.at[peer], grp=peer
        ).wait_recv()
    for turn in range(rounds):
        rows = pl.ds(turn * STEP, STEP)
        swapped = swap[...].reshape(tile, tile)[turn * STEP : (turn + 1) * STEP]
        mixed = (
            2.0 * amp[0, 0, rows].astype(jnp.float32) - swapped.astype(jnp.float32)
        )
        mixed_t[turn] = mixed.T.astype(jnp.bfloat16)
        to_workers(lambda worker_side: mix_copy(turn, worker_side).start())

        @pl.when(works)
        def _():
            got_t[turn, mem] = mixed_t[turn, own_rows]

    @pl.when(works)
    def _():
        tasks_in.wait()
        counts_in.wait()
        owner_in.wait()
        half_in.wait()
        spread[...] = spread_counts(members, tasks, counts, owner)
        for source in range(members):
            @pl.when(mem != source)
            def _():
                remote(
                    halves.at[source], halves.at[source],
                    int_ss.at[0], int_rs.at[source], mem=partner,
                ).wait_recv()

        def weigh(index, carry):
            rows = pl.ds(pl.multiple_of(index * BAND, BAND), BAND)
            sums = jnp.dot(
                spread[...], halves[:, rows].reshape(members * BAND, tile),
                preferred_element_type=jnp.float32,
            )
            weighed[:, :, rows] = sums.astype(jnp.bfloat16).reshape(members, members, BAND, tile)
            return carry

        lax.fori_loop(0, half // BAND, weigh, 0)

        def finish(turn):
            for row in range(planes):
                part_copy(turn, row).wait_recv()
                final[turn, row] = (
                    kept[turn, row] + taken[turn, row].astype(jnp.float32)
                ).astype(jnp.bfloat16)

                @pl.when(plane != row)
                def _():
                    out_copy(turn, row).start()

                @pl.when(plane == row)
                def _():
                    own_copy(turn).start()

        for turn in range(rounds):
            for source in range(members):
                @pl.when(mem != source)
                def _():
                    remote(
                        got_t.at[turn, source], got_t.at[turn, source],
                        mix_ss.at[turn, 0], mix_rs.at[turn, source], mem=partner,
                    ).wait_recv()
            left = got_t[turn].reshape(members * half, STEP).T

            def multiply(target):
                return jnp.dot(
                    left, weighed[target].reshape(members * half, tile),
                    preferred_element_type=jnp.float32,
                )

            for row in range(planes):
                given[turn, row] = multiply(row * 2 + 1 - side).astype(jnp.bfloat16)
                part_copy(turn, row).start()
            for row in range(planes):
                kept[turn, row] = multiply(row * 2 + side)
            if turn:
                finish(turn - 1)
        finish(rounds - 1)
        for turn in range(rounds):
            own_copy(turn).wait()
            for row in range(planes):
                part_copy(turn, row).wait_send()

                @pl.when(plane != row)
                def _():
                    out_copy(turn, row).wait_send()

    @pl.when(jnp.logical_not(works))
    def _():
        for turn in range(rounds):
            out_copy(turn, 0).wait_recv()

    for turn in range(1, groups):
        swap_copy(lax.rem(grp + turn, groups)).wait_send()
    to_workers(lambda worker_side: int_copy(worker_side).wait_send())
    for turn in range(rounds):
        to_workers(lambda worker_side: mix_copy(turn, worker_side).wait_send())


def local_workers(amplitudes, integrals, task_list, task_counts, owner_map):
    groups, members = lax.axis_size("grp"), lax.axis_size("mem")
    tile = amplitudes.shape[-1]
    half, rounds, planes = tile // 2, tile // STEP, members // 2
    hbm = pl.BlockSpec(memory_space=pltpu.HBM)
    dma = pltpu.SemaphoreType.DMA
    bf16 = jnp.bfloat16
    return pl.pallas_call(
        functools.partial(cycle_kernel, groups, members),
        out_shape=jax.ShapeDtypeStruct(amplitudes.shape, bf16),
        in_specs=[hbm] * 5,
        out_specs=hbm,
        scratch_shapes=[
            pltpu.VMEM(amplitudes.shape, bf16),
            pltpu.VMEM((3, 1, task_list.shape[1]), jnp.int32),
            pltpu.SMEM(task_counts.shape, jnp.int32),
            pltpu.SMEM(owner_map.shape, jnp.int32),
            pltpu.VMEM((groups, tile // groups, tile), bf16),
            pltpu.VMEM((members, half, tile), bf16),
            pltpu.VMEM((rounds, tile, STEP), bf16),
            pltpu.VMEM((rounds, members, half, STEP), bf16),
            pltpu.VMEM((members, members, half, tile), bf16),
            pltpu.VMEM((rounds, planes, STEP, tile), bf16),
            pltpu.VMEM((rounds, planes, STEP, tile), bf16),
            pltpu.VMEM((rounds, planes, STEP, tile), jnp.float32),
            pltpu.VMEM((rounds, planes, STEP, tile), bf16),
            pltpu.VMEM((members * members * BAND, members * BAND), bf16),
            dma((groups,)), dma((groups,)),
            dma((2,)), dma((members,)),
            dma((rounds, 2)), dma((rounds, members)),
            dma((rounds, planes)), dma((rounds, planes)),
            dma((rounds, planes)), dma((rounds,)),
            dma((5,)),
        ],
        compiler_params=pltpu.CompilerParams(
            collective_id=0, has_side_effects=True, vmem_limit_bytes=VMEM_BYTES
        ),
    )(amplitudes, integrals, jnp.transpose(task_list, (2, 0, 1)), task_counts, owner_map)


def solution(mesh):
    placed = (
        P("grp", "mem", None, None),
        P("grp", "mem", None, None),
        P("grp", None, None),
        P("grp", None),
        P(),
    )
    body = local_workers if mesh.shape["mem"] == 2 * 4 else local
    return jax.shard_map(
        body, mesh=mesh, in_specs=placed, out_specs=P("grp", "mem", None, None), check_vma=False
    )
```

```python
import functools
import math

import jax
import jax.numpy as jnp
from jax import lax
from jax.experimental import pallas as pl
from jax.experimental.pallas import tpu as pltpu
from jax.sharding import PartitionSpec as P

TASK_DEV = 64


def block_products(got_mixed, got_int, picked, living):
    left_tile = jnp.take(got_mixed, picked[:, 1], axis=0)
    right_tile = jnp.take(got_int, picked[:, 2], axis=0)
    product = jnp.einsum("kxy,kyz->kxz", left_tile, right_tile, preferred_element_type=jnp.float32)
    return jnp.where(living[:, None, None], product, jnp.float32(0.0))


def add_targets(running, targets, living, product):
    safe_targets = jnp.where(living, targets, 0)
    return running.at[safe_targets].add(product)


def local(amplitudes, integrals, task_list, task_counts, owner_map):
    tile_order = amplitudes.shape[-1]
    members = lax.axis_size("mem")
    device = lax.axis_index("mem")
    slot_count = TASK_DEV
    own_amp = amplitudes[0, 0]
    swapped = lax.all_to_all(own_amp, "grp", split_axis=0, concat_axis=0, tiled=True)
    mixed_tile = (2.0 * own_amp.astype(jnp.float32) - swapped.astype(jnp.float32)).astype(
        jnp.bfloat16
    )
    own_int = integrals[0, 0]
    holders = jnp.take(owner_map, task_list[0], axis=0)
    live_all = jnp.arange(slot_count, dtype=jnp.int32)[None, :] < task_counts[0][:, None]
    got_mixed, got_int = (
        lax.all_gather(mixed_tile[None], "mem", axis=0, tiled=True),
        lax.all_gather(own_int[None], "mem", axis=0, tiled=True),
    )
    flat_live = live_all.reshape(-1)
    mine = flat_live & (holders[:, 0] == device)
    order = jnp.argsort(jnp.where(mine, 0, 1).astype(jnp.int32), stable=True)
    total_mine = jnp.sum(mine.astype(jnp.int32))
    block_size = math.gcd(members * slot_count, 16)
    block_count = (total_mine + block_size - 1) // block_size
    slot_index = jnp.arange(block_size, dtype=jnp.int32)

    def owner_step(state):
        turn, per_exec = state
        first = turn * block_size
        chosen = lax.dynamic_slice_in_dim(order, first, block_size, 0)
        picked = jnp.take(holders, chosen, axis=0)
        living = slot_index + first < total_mine
        product = block_products(got_mixed, got_int, picked, living)
        return (turn + 1, add_targets(per_exec, chosen // slot_count, living, product))

    start_exec = jnp.zeros((members, tile_order, tile_order), jnp.float32)
    _, per_exec = lax.while_loop(
        lambda state: state[0] < block_count, owner_step, (jnp.int32(0), start_exec)
    )
    summed = jnp.sum(per_exec.astype(jnp.bfloat16), axis=0, dtype=jnp.float32)
    return summed.astype(jnp.bfloat16)[None, None]


MESH = pl.DeviceIdType.MESH
STEP = 64
PIECE = 128
BAND = 32
VMEM_BYTES = 65280 * 1024


def remote(src, dst, send_sem, recv_sem, **place):
    return pltpu.make_async_remote_copy(
        src_ref=src, dst_ref=dst, send_sem=send_sem, recv_sem=recv_sem,
        device_id=place, device_id_type=MESH,
    )


def spread_counts(members, tasks, counts, owner):
    total = tasks.shape[-1]
    slots = total // members
    ids = [tasks[field] for field in range(3)]
    rows = [jnp.zeros((1, total), jnp.int32) for _ in range(3)]
    for tile_id in range(members):
        row = owner[tile_id]
        rows = [jnp.where(ids[f] == tile_id, row, rows[f]) for f in range(3)]
    place = lax.broadcasted_iota(jnp.int32, (1, total), 1)
    live = jnp.zeros((1, total), jnp.int32)
    for executor in range(members):
        offset = place - executor * slots
        inside = (offset >= 0) & (offset < jnp.minimum(counts[0, executor], slots))
        live = jnp.where(inside, 1, live)
    key = rows[2] * members + rows[0]
    key = jnp.where(live == 1, key, -1)
    tall, wide = members * members * BAND, members * BAND
    hot_left = lax.broadcasted_iota(jnp.int32, (tall, total), 0) // BAND == key
    hot_right = lax.broadcasted_iota(jnp.int32, (wide, total), 0) // BAND == rows[1]
    spread = lax.dot_general(
        jnp.where(hot_left, 1.0, 0.0).astype(jnp.bfloat16),
        jnp.where(hot_right, 1.0, 0.0).astype(jnp.bfloat16),
        (((1,), (1,)), ((), ())),
        preferred_element_type=jnp.float32,
    )
    down = lax.broadcasted_iota(jnp.int32, (tall, wide), 0) % BAND
    across = lax.broadcasted_iota(jnp.int32, (tall, wide), 1) % BAND
    return jnp.where(down == across, spread, 0.0).astype(jnp.bfloat16)


def cycle_kernel(
    groups, members,
    amp_hbm, integ, tasks_hbm, counts_hbm, owner_hbm, out,
    amp, tasks, counts, owner,
    swap, mixed, got_int, got_mix, weighed, final, spread,
    swap_ss, swap_rs, int_ss, int_rs, pass_ss, mix_ss, mix_rs, out_ss, out_rs, own_sem, local_sem,
):
    grp, mem = lax.axis_index("grp"), lax.axis_index("mem")
    tile = amp.shape[-1]
    half, block, planes = tile // 2, tile // groups, members // 2
    rounds, pieces = half // STEP, tile // PIECE
    plane, side = lax.div(mem, 2), lax.rem(mem, 2)
    partner = mem + 1 - 2 * side
    work_plane = planes // 2 - 1 + lax.rem(grp, 2)
    works = plane == work_plane

    amp_in = pltpu.make_async_copy(amp_hbm, amp, local_sem.at[0])
    tasks_in = pltpu.make_async_copy(tasks_hbm, tasks, local_sem.at[1])
    counts_in = pltpu.make_async_copy(counts_hbm, counts, local_sem.at[2])
    owner_in = pltpu.make_async_copy(owner_hbm, owner, local_sem.at[3])
    int_in = pltpu.make_async_copy(integ.at[0, 0], got_int.at[mem], local_sem.at[4])
    amp_in.start()

    @pl.when(works)
    def _():
        tasks_in.start()
        counts_in.start()
        owner_in.start()
        int_in.start()

    barrier = pltpu.get_barrier_semaphore()
    for turn in range(1, groups):
        pl.semaphore_signal(
            barrier, inc=1, device_id={"grp": lax.rem(grp + turn, groups)}, device_id_type=MESH
        )

    @pl.when(works)
    def _():
        for turn in range(1, members):
            pl.semaphore_signal(
                barrier, inc=1, device_id={"mem": lax.rem(mem + turn, members)}, device_id_type=MESH
            )
        pl.semaphore_wait(barrier, groups + members - 2)

    @pl.when(jnp.logical_not(works))
    def _():
        for worker_side in range(2):
            pl.semaphore_signal(
                barrier, inc=1, device_id={"mem": work_plane * 2 + worker_side}, device_id_type=MESH
            )
        pl.semaphore_wait(barrier, groups + 1)

    def swap_copy(peer):
        return remote(
            amp_hbm.at[0, 0, pl.ds(pl.multiple_of(peer * block, block), block)],
            swap.at[grp], swap_ss.at[peer], swap_rs.at[grp], grp=peer,
        )

    def int_copy(piece):
        rows = pl.ds(piece * PIECE, PIECE)
        return remote(
            integ.at[0, 0, rows], got_int.at[mem, rows], int_ss.at[piece], int_rs.at[piece, mem],
            mem=jnp.where(works, partner, work_plane * 2 + side),
        )

    def pass_copy(piece, row):
        source, rows = row * 2 + side, pl.ds(piece * PIECE, PIECE)
        return remote(
            got_int.at[source, rows], got_int.at[source, rows],
            pass_ss.at[piece, row], int_rs.at[piece, source], mem=partner,
        )

    def int_arrival(piece, source):
        rows = pl.ds(piece * PIECE, PIECE)
        return remote(
            got_int.at[source, rows], got_int.at[source, rows],
            int_ss.at[piece], int_rs.at[piece, source], mem=partner,
        )

    def mix_copy(turn, worker_side):
        return remote(
            mixed.at[pl.ds(worker_side * half + turn * STEP, STEP)],
            got_mix.at[turn, mem], mix_ss.at[turn, worker_side], mix_rs.at[turn, mem],
            mem=work_plane * 2 + worker_side,
        )

    def out_rows(turn, worker_side):
        return pl.ds(pl.multiple_of(worker_side * half + turn * STEP, STEP), STEP)

    def out_copy(turn, target):
        return remote(
            final.at[turn, target], out.at[0, 0, out_rows(turn, side)],
            out_ss.at[turn, target], out_rs.at[turn, side], mem=target,
        )

    def out_arrival(turn, worker_side):
        return remote(
            final.at[turn, 0], out.at[0, 0, out_rows(turn, worker_side)],
            out_ss.at[turn, 0], out_rs.at[turn, worker_side], mem=partner,
        )

    def own_copy(turn):
        return pltpu.make_async_copy(
            final.at[turn, mem], out.at[0, 0, out_rows(turn, side)], own_sem.at[turn]
        )

    def to_workers(do):
        for worker_side in range(2):
            @pl.when(mem != work_plane * 2 + worker_side)
            def _():
                do(worker_side)

    for turn in range(1, groups):
        swap_copy(lax.rem(grp + turn, groups)).start()
    for piece in range(pieces):
        int_copy(piece).start()

    amp_in.wait()
    own_block = pl.ds(pl.multiple_of(grp * block, block), block)
    swap[grp] = amp[0, 0, own_block]

    for turn in range(1, groups):
        peer = lax.rem(grp + turn, groups)
        remote(
            swap.at[peer], swap.at[peer], swap_ss.at[peer], swap_rs.at[peer], grp=peer
        ).wait_recv()
    for turn in range(rounds):
        for worker_side in range(2):
            first = worker_side * half + turn * STEP
            rows = pl.ds(first, STEP)
            swapped = swap[...].reshape(tile, tile)[first : first + STEP]
            mixed[rows] = (
                2.0 * amp[0, 0, rows].astype(jnp.float32) - swapped.astype(jnp.float32)
            ).astype(jnp.bfloat16)
        to_workers(lambda worker_side: mix_copy(turn, worker_side).start())

    @pl.when(works)
    def _():
        for piece in range(pieces):
            for row in range(planes):
                @pl.when(plane != row)
                def _():
                    int_arrival(piece, row * 2 + side).wait_recv()
                    pass_copy(piece, row).start()

        tasks_in.wait()
        counts_in.wait()
        owner_in.wait()
        spread[...] = spread_counts(members, tasks, counts, owner)
        for turn in range(rounds):
            got_mix[turn, mem] = mixed[out_rows(turn, side)]

        for turn in range(rounds):
            for source in range(members):
                @pl.when(mem != source)
                def _():
                    remote(
                        got_mix.at[turn, source], got_mix.at[turn, source],
                        mix_ss.at[turn, 0], mix_rs.at[turn, source], mem=partner,
                    ).wait_recv()
            for band in range(STEP // BAND):
                rows = pl.ds(band * BAND, BAND)
                read = got_mix[turn, :, rows].reshape(members * BAND, tile)
                for b in range(members):
                    sums = jnp.dot(
                        spread[pl.ds(b * members * BAND, members * BAND)], read,
                        preferred_element_type=jnp.float32,
                    )
                    weighed[:, rows, pl.ds(b * tile, tile)] = sums.astype(jnp.bfloat16).reshape(
                        members, BAND, tile
                    )
            if turn == 0:
                int_in.wait()
                for piece in range(pieces):
                    for row in range(planes):
                        int_arrival(piece, row * 2 + 1 - side).wait_recv()
            product = jnp.dot(
                weighed[...].reshape(members * STEP, members * tile),
                got_int[...].reshape(members * tile, tile),
                preferred_element_type=jnp.float32,
            )
            final[turn] = product.astype(jnp.bfloat16).reshape(members, STEP, tile)
            for target in range(members):
                @pl.when(mem != target)
                def _():
                    out_copy(turn, target).start()
            own_copy(turn).start()

        for turn in range(rounds):
            own_copy(turn).wait()
            out_arrival(turn, 1 - side).wait_recv()
            for target in range(members):
                @pl.when(mem != target)
                def _():
                    out_copy(turn, target).wait_send()
        for piece in range(pieces):
            for row in range(planes):
                @pl.when(plane != row)
                def _():
                    pass_copy(piece, row).wait_send()

    @pl.when(jnp.logical_not(works))
    def _():
        for turn in range(rounds):
            for worker_side in range(2):
                out_arrival(turn, worker_side).wait_recv()

    for turn in range(1, groups):
        swap_copy(lax.rem(grp + turn, groups)).wait_send()
    for piece in range(pieces):
        int_copy(piece).wait_send()
    for turn in range(rounds):
        to_workers(lambda worker_side: mix_copy(turn, worker_side).wait_send())


def local_workers(amplitudes, integrals, task_list, task_counts, owner_map):
    groups, members = lax.axis_size("grp"), lax.axis_size("mem")
    tile = amplitudes.shape[-1]
    rounds, pieces, planes = tile // 2 // STEP, tile // PIECE, members // 2
    hbm = pl.BlockSpec(memory_space=pltpu.HBM)
    dma = pltpu.SemaphoreType.DMA
    bf16 = jnp.bfloat16
    return pl.pallas_call(
        functools.partial(cycle_kernel, groups, members),
        out_shape=jax.ShapeDtypeStruct(amplitudes.shape, bf16),
        in_specs=[hbm] * 5,
        out_specs=hbm,
        scratch_shapes=[
            pltpu.VMEM(amplitudes.shape, bf16),
            pltpu.VMEM((3, 1, task_list.shape[1]), jnp.int32),
            pltpu.SMEM(task_counts.shape, jnp.int32),
            pltpu.SMEM(owner_map.shape, jnp.int32),
            pltpu.VMEM((groups, tile // groups, tile), bf16),
            pltpu.VMEM((tile, tile), bf16),
            pltpu.VMEM((members, tile, tile), bf16),
            pltpu.VMEM((rounds, members, STEP, tile), bf16),
            pltpu.VMEM((members, STEP, members * tile), bf16),
            pltpu.VMEM((rounds, members, STEP, tile), bf16),
            pltpu.VMEM((members * members * BAND, members * BAND), bf16),
            dma((groups,)), dma((groups,)),
            dma((pieces,)), dma((pieces, members)), dma((pieces, planes)),
            dma((rounds, 2)), dma((rounds, members)),
            dma((rounds, members)), dma((rounds, 2)), dma((rounds,)),
            dma((5,)),
        ],
        compiler_params=pltpu.CompilerParams(
            collective_id=0, has_side_effects=True, vmem_limit_bytes=VMEM_BYTES
        ),
    )(amplitudes, integrals, jnp.transpose(task_list, (2, 0, 1)), task_counts, owner_map)


def solution(mesh):
    placed = (
        P("grp", "mem", None, None),
        P("grp", "mem", None, None),
        P("grp", None, None),
        P("grp", None),
        P(),
    )
    body = local_workers if mesh.shape["mem"] == 2 * 4 else local
    return jax.shard_map(
        body, mesh=mesh, in_specs=placed, out_specs=P("grp", "mem", None, None), check_vma=False
    )
```

```python
import functools
import math

import jax
import jax.numpy as jnp
from jax import lax
from jax.experimental import pallas as pl
from jax.experimental.pallas import tpu as pltpu
from jax.sharding import PartitionSpec as P

TASK_DEV = 64


def block_products(got_mixed, got_int, picked, living):
    left_tile = jnp.take(got_mixed, picked[:, 1], axis=0)
    right_tile = jnp.take(got_int, picked[:, 2], axis=0)
    product = jnp.einsum("kxy,kyz->kxz", left_tile, right_tile, preferred_element_type=jnp.float32)
    return jnp.where(living[:, None, None], product, jnp.float32(0.0))


def add_targets(running, targets, living, product):
    safe_targets = jnp.where(living, targets, 0)
    return running.at[safe_targets].add(product)


def local(amplitudes, integrals, task_list, task_counts, owner_map):
    tile_order = amplitudes.shape[-1]
    members = lax.axis_size("mem")
    device = lax.axis_index("mem")
    slot_count = TASK_DEV
    own_amp = amplitudes[0, 0]
    swapped = lax.all_to_all(own_amp, "grp", split_axis=0, concat_axis=0, tiled=True)
    mixed_tile = (2.0 * own_amp.astype(jnp.float32) - swapped.astype(jnp.float32)).astype(
        jnp.bfloat16
    )
    own_int = integrals[0, 0]
    holders = jnp.take(owner_map, task_list[0], axis=0)
    live_all = jnp.arange(slot_count, dtype=jnp.int32)[None, :] < task_counts[0][:, None]
    got_mixed, got_int = (
        lax.all_gather(mixed_tile[None], "mem", axis=0, tiled=True),
        lax.all_gather(own_int[None], "mem", axis=0, tiled=True),
    )
    flat_live = live_all.reshape(-1)
    mine = flat_live & (holders[:, 0] == device)
    order = jnp.argsort(jnp.where(mine, 0, 1).astype(jnp.int32), stable=True)
    total_mine = jnp.sum(mine.astype(jnp.int32))
    block_size = math.gcd(members * slot_count, 16)
    block_count = (total_mine + block_size - 1) // block_size
    slot_index = jnp.arange(block_size, dtype=jnp.int32)

    def owner_step(state):
        turn, per_exec = state
        first = turn * block_size
        chosen = lax.dynamic_slice_in_dim(order, first, block_size, 0)
        picked = jnp.take(holders, chosen, axis=0)
        living = slot_index + first < total_mine
        product = block_products(got_mixed, got_int, picked, living)
        return (turn + 1, add_targets(per_exec, chosen // slot_count, living, product))

    start_exec = jnp.zeros((members, tile_order, tile_order), jnp.float32)
    _, per_exec = lax.while_loop(
        lambda state: state[0] < block_count, owner_step, (jnp.int32(0), start_exec)
    )
    summed = jnp.sum(per_exec.astype(jnp.bfloat16), axis=0, dtype=jnp.float32)
    return summed.astype(jnp.bfloat16)[None, None]


MESH = pl.DeviceIdType.MESH
STEP = 128
BAND = 32
VMEM_BYTES = 65280 * 1024


def remote(src, dst, send_sem, recv_sem, **place):
    return pltpu.make_async_remote_copy(
        src_ref=src, dst_ref=dst, send_sem=send_sem, recv_sem=recv_sem,
        device_id=place, device_id_type=MESH,
    )


def spread_counts(members, tasks, counts, owner):
    total = tasks.shape[-1]
    slots = total // members
    ids = [tasks[field] for field in range(3)]
    rows = [jnp.zeros((1, total), jnp.int32) for _ in range(3)]
    for tile_id in range(members):
        row = owner[tile_id]
        rows = [jnp.where(ids[f] == tile_id, row, rows[f]) for f in range(3)]
    place = lax.broadcasted_iota(jnp.int32, (1, total), 1)
    live = jnp.zeros((1, total), jnp.int32)
    for executor in range(members):
        offset = place - executor * slots
        inside = (offset >= 0) & (offset < jnp.minimum(counts[0, executor], slots))
        live = jnp.where(inside, 1, live)
    key = rows[0] * members + rows[1]
    key = jnp.where(live == 1, key, -1)
    tall, wide = members * members * BAND, members * BAND
    hot_left = lax.broadcasted_iota(jnp.int32, (tall, total), 0) // BAND == key
    hot_right = lax.broadcasted_iota(jnp.int32, (wide, total), 0) // BAND == rows[2]
    spread = lax.dot_general(
        jnp.where(hot_left, 1.0, 0.0).astype(jnp.bfloat16),
        jnp.where(hot_right, 1.0, 0.0).astype(jnp.bfloat16),
        (((1,), (1,)), ((), ())),
        preferred_element_type=jnp.float32,
    )
    down = lax.broadcasted_iota(jnp.int32, (tall, wide), 0) % BAND
    across = lax.broadcasted_iota(jnp.int32, (tall, wide), 1) % BAND
    return jnp.where(down == across, spread, 0.0).astype(jnp.bfloat16)


def cycle_kernel(
    groups, members,
    amp_hbm, integ, tasks_hbm, counts_hbm, owner_hbm, out,
    amp, tasks, counts, owner,
    swap, halves, mixed_t, got_t, weighed, given, taken, kept, final, landed, passing, spread,
    swap_ss, swap_rs, int_ss, int_rs, mix_ss, mix_rs, part_ss, part_rs, out_ss, out_rs, pass_ss, pass_rs, local_sem,
):
    grp, mem = lax.axis_index("grp"), lax.axis_index("mem")
    tile = amp.shape[-1]
    half, block, rounds, planes = tile // 2, tile // groups, tile // STEP, members // 2
    plane, side = lax.div(mem, 2), lax.rem(mem, 2)
    partner = mem + 1 - 2 * side
    work_plane = planes // 2 - 1 + lax.rem(grp, 2)
    works = plane == work_plane
    outer_plane = lax.rem(grp, 2) * (planes - 1)
    adds = plane == outer_plane
    own_rows = pl.ds(pl.multiple_of(side * half, half), half)

    amp_in = pltpu.make_async_copy(amp_hbm, amp, local_sem.at[0])
    tasks_in = pltpu.make_async_copy(tasks_hbm, tasks, local_sem.at[1])
    counts_in = pltpu.make_async_copy(counts_hbm, counts, local_sem.at[2])
    owner_in = pltpu.make_async_copy(owner_hbm, owner, local_sem.at[3])
    half_in = pltpu.make_async_copy(integ.at[0, 0, own_rows], halves.at[mem], local_sem.at[4])
    amp_in.start()

    @pl.when(works)
    def _():
        tasks_in.start()
        counts_in.start()
        owner_in.start()
        half_in.start()

    barrier = pltpu.get_barrier_semaphore()
    for turn in range(1, groups):
        pl.semaphore_signal(
            barrier, inc=1, device_id={"grp": lax.rem(grp + turn, groups)}, device_id_type=MESH
        )

    @pl.when(works)
    def _():
        for turn in range(1, members):
            pl.semaphore_signal(
                barrier, inc=1, device_id={"mem": lax.rem(mem + turn, members)}, device_id_type=MESH
            )
        pl.semaphore_wait(barrier, groups + members - 2)

    @pl.when(jnp.logical_not(works))
    def _():
        for worker_side in range(2):
            pl.semaphore_signal(
                barrier, inc=1, device_id={"mem": work_plane * 2 + worker_side}, device_id_type=MESH
            )
        pl.semaphore_signal(barrier, inc=1, device_id={"mem": partner}, device_id_type=MESH)
        pl.semaphore_wait(barrier, groups + 2)

    def swap_copy(peer):
        return remote(
            amp_hbm.at[0, 0, pl.ds(pl.multiple_of(peer * block, block), block)],
            swap.at[grp], swap_ss.at[peer], swap_rs.at[grp], grp=peer,
        )

    def int_copy(worker_side):
        return remote(
            integ.at[0, 0, pl.ds(worker_side * half, half)],
            halves.at[mem], int_ss.at[worker_side], int_rs.at[mem],
            mem=work_plane * 2 + worker_side,
        )

    def mix_copy(turn, worker_side):
        return remote(
            mixed_t.at[turn, pl.ds(worker_side * half, half)],
            got_t.at[turn, mem], mix_ss.at[turn, worker_side], mix_rs.at[turn, mem],
            mem=work_plane * 2 + worker_side,
        )

    def part_copy(turn, row):
        return remote(
            given.at[turn, row], taken.at[turn, row],
            part_ss.at[turn, row], part_rs.at[turn, row], mem=partner,
        )

    def outer_copy(turn, kind):
        return remote(
            final.at[turn, outer_plane] if kind == 0 else given.at[turn, outer_plane],
            landed.at[turn, side] if kind == 0 else passing.at[turn],
            pass_ss.at[turn, kind], pass_rs.at[turn, side if kind == 0 else 2],
            mem=outer_plane * 2 + side,
        )

    def pass_copy(turn):
        return remote(
            passing.at[turn], landed.at[turn, side],
            pass_ss.at[turn, 0], pass_rs.at[turn, side], mem=partner,
        )

    def out_copy(turn, row):
        return remote(
            final.at[turn, row], out.at[0, 0, pl.ds(turn * STEP, STEP)],
            out_ss.at[turn, row], out_rs.at[turn], mem=row * 2 + side,
        )

    def own_copy(turn):
        return pltpu.make_async_copy(
            final.at[turn, plane], out.at[0, 0, pl.ds(turn * STEP, STEP)], out_rs.at[turn],
        )

    def to_workers(do):
        for worker_side in range(2):
            @pl.when(mem != work_plane * 2 + worker_side)
            def _():
                do(worker_side)

    for turn in range(1, groups):
        swap_copy(lax.rem(grp + turn, groups)).start()
    to_workers(lambda worker_side: int_copy(worker_side).start())

    amp_in.wait()
    own_block = pl.ds(pl.multiple_of(grp * block, block), block)
    swap[grp] = amp[0, 0, own_block]

    for turn in range(1, groups):
        peer = lax.rem(grp + turn, groups)
        remote(
            swap.at[peer], swap.at[peer], swap_ss.at[peer], swap_rs.at[peer], grp=peer
        ).wait_recv()
    for turn in range(rounds):
        rows = pl.ds(turn * STEP, STEP)
        swapped = swap[...].reshape(tile, tile)[turn * STEP : (turn + 1) * STEP]
        mixed = (
            2.0 * amp[0, 0, rows].astype(jnp.float32) - swapped.astype(jnp.float32)
        )
        mixed_t[turn] = mixed.T.astype(jnp.bfloat16)
        to_workers(lambda worker_side: mix_copy(turn, worker_side).start())

        @pl.when(works)
        def _():
            got_t[turn, mem] = mixed_t[turn, own_rows]

    @pl.when(works)
    def _():
        tasks_in.wait()
        counts_in.wait()
        owner_in.wait()
        half_in.wait()
        spread[...] = spread_counts(members, tasks, counts, owner)
        for source in range(members):
            @pl.when(mem != source)
            def _():
                remote(
                    halves.at[source], halves.at[source],
                    int_ss.at[0], int_rs.at[source], mem=partner,
                ).wait_recv()

        def weigh(index, carry):
            rows = pl.ds(pl.multiple_of(index * BAND, BAND), BAND)
            sums = jnp.dot(
                spread[...], halves[:, rows].reshape(members * BAND, tile),
                preferred_element_type=jnp.float32,
            )
            weighed[:, :, rows] = sums.astype(jnp.bfloat16).reshape(members, members, BAND, tile)
            return carry

        lax.fori_loop(0, half // BAND, weigh, 0)

        def finish(turn):
            for row in range(planes):
                @pl.when(outer_plane != row)
                def _():
                    part_copy(turn, row).wait_recv()
                    final[turn, row] = (
                        kept[turn, row] + taken[turn, row].astype(jnp.float32)
                    ).astype(jnp.bfloat16)

                @pl.when((outer_plane != row) & (plane != row))
                def _():
                    out_copy(turn, row).start()

                @pl.when(plane == row)
                def _():
                    own_copy(turn).start()

        for turn in range(rounds):
            for source in range(members):
                @pl.when(mem != source)
                def _():
                    remote(
                        got_t.at[turn, source], got_t.at[turn, source],
                        mix_ss.at[turn, 0], mix_rs.at[turn, source], mem=partner,
                    ).wait_recv()
            left = got_t[turn].reshape(members * half, STEP).T

            def multiply(target):
                return jnp.dot(
                    left, weighed[target].reshape(members * half, tile),
                    preferred_element_type=jnp.float32,
                )

            given[turn, outer_plane] = multiply(outer_plane * 2 + 1 - side).astype(jnp.bfloat16)
            outer_copy(turn, 1).start()
            for row in range(planes):
                @pl.when(outer_plane != row)
                def _():
                    given[turn, row] = multiply(row * 2 + 1 - side).astype(jnp.bfloat16)
                    part_copy(turn, row).start()
            final[turn, outer_plane] = multiply(outer_plane * 2 + side).astype(jnp.bfloat16)
            outer_copy(turn, 0).start()
            for row in range(planes):
                @pl.when(outer_plane != row)
                def _():
                    kept[turn, row] = multiply(row * 2 + side)
            if turn:
                finish(turn - 1)
        finish(rounds - 1)
        for turn in range(rounds):
            own_copy(turn).wait()
            for kind in range(2):
                outer_copy(turn, kind).wait_send()
            for row in range(planes):
                @pl.when(outer_plane != row)
                def _():
                    part_copy(turn, row).wait_send()

                @pl.when((outer_plane != row) & (plane != row))
                def _():
                    out_copy(turn, row).wait_send()

    @pl.when(jnp.logical_not(works | adds))
    def _():
        for turn in range(rounds):
            out_copy(turn, 0).wait_recv()

    @pl.when(adds)
    def _():
        def pass_arrival(turn, kind):
            target = passing.at[turn] if kind == 2 else landed.at[turn, kind]
            return remote(
                target, target, pass_ss.at[turn, 0], pass_rs.at[turn, kind], mem=partner
            )

        def add(turn):
            for worker_side in range(2):
                pass_arrival(turn, worker_side).wait_recv()
            final[turn, plane] = (
                landed[turn, 0].astype(jnp.float32) + landed[turn, 1].astype(jnp.float32)
            ).astype(jnp.bfloat16)
            own_copy(turn).start()

        for turn in range(rounds):
            pass_arrival(turn, 2).wait_recv()
            pass_copy(turn).start()
            if turn:
                add(turn - 1)
        add(rounds - 1)
        for turn in range(rounds):
            pass_copy(turn).wait_send()
            own_copy(turn).wait()

    for turn in range(1, groups):
        swap_copy(lax.rem(grp + turn, groups)).wait_send()
    to_workers(lambda worker_side: int_copy(worker_side).wait_send())
    for turn in range(rounds):
        to_workers(lambda worker_side: mix_copy(turn, worker_side).wait_send())


def local_workers(amplitudes, integrals, task_list, task_counts, owner_map):
    groups, members = lax.axis_size("grp"), lax.axis_size("mem")
    tile = amplitudes.shape[-1]
    half, rounds, planes = tile // 2, tile // STEP, members // 2
    hbm = pl.BlockSpec(memory_space=pltpu.HBM)
    dma = pltpu.SemaphoreType.DMA
    bf16 = jnp.bfloat16
    return pl.pallas_call(
        functools.partial(cycle_kernel, groups, members),
        out_shape=jax.ShapeDtypeStruct(amplitudes.shape, bf16),
        in_specs=[hbm] * 5,
        out_specs=hbm,
        scratch_shapes=[
            pltpu.VMEM(amplitudes.shape, bf16),
            pltpu.VMEM((3, 1, task_list.shape[1]), jnp.int32),
            pltpu.SMEM(task_counts.shape, jnp.int32),
            pltpu.SMEM(owner_map.shape, jnp.int32),
            pltpu.VMEM((groups, tile // groups, tile), bf16),
            pltpu.VMEM((members, half, tile), bf16),
            pltpu.VMEM((rounds, tile, STEP), bf16),
            pltpu.VMEM((rounds, members, half, STEP), bf16),
            pltpu.VMEM((members, members, half, tile), bf16),
            pltpu.VMEM((rounds, planes, STEP, tile), bf16),
            pltpu.VMEM((rounds, planes, STEP, tile), bf16),
            pltpu.VMEM((rounds, planes, STEP, tile), jnp.float32),
            pltpu.VMEM((rounds, planes, STEP, tile), bf16),
            pltpu.VMEM((rounds, 2, STEP, tile), bf16),
            pltpu.VMEM((rounds, STEP, tile), bf16),
            pltpu.VMEM((members * members * BAND, members * BAND), bf16),
            dma((groups,)), dma((groups,)),
            dma((2,)), dma((members,)),
            dma((rounds, 2)), dma((rounds, members)),
            dma((rounds, planes)), dma((rounds, planes)),
            dma((rounds, planes)), dma((rounds,)),
            dma((rounds, 2)), dma((rounds, 3)),
            dma((5,)),
        ],
        compiler_params=pltpu.CompilerParams(
            collective_id=0, has_side_effects=True, vmem_limit_bytes=VMEM_BYTES
        ),
    )(amplitudes, integrals, jnp.transpose(task_list, (2, 0, 1)), task_counts, owner_map)


def solution(mesh):
    placed = (
        P("grp", "mem", None, None),
        P("grp", "mem", None, None),
        P("grp", None, None),
        P("grp", None),
        P(),
    )
    body = local_workers if mesh.shape["mem"] == 2 * 4 else local
    return jax.shard_map(
        body, mesh=mesh, in_specs=placed, out_specs=P("grp", "mem", None, None), check_vma=False
    )
```

```python
import functools
import math

import jax
import jax.numpy as jnp
from jax import lax
from jax.experimental import pallas as pl
from jax.experimental.pallas import tpu as pltpu
from jax.sharding import PartitionSpec as P

TASK_DEV = 64


def block_products(got_mixed, got_int, picked, living):
    left_tile = jnp.take(got_mixed, picked[:, 1], axis=0)
    right_tile = jnp.take(got_int, picked[:, 2], axis=0)
    product = jnp.einsum("kxy,kyz->kxz", left_tile, right_tile, preferred_element_type=jnp.float32)
    return jnp.where(living[:, None, None], product, jnp.float32(0.0))


def add_targets(running, targets, living, product):
    safe_targets = jnp.where(living, targets, 0)
    return running.at[safe_targets].add(product)


def local(amplitudes, integrals, task_list, task_counts, owner_map):
    tile_order = amplitudes.shape[-1]
    members = lax.axis_size("mem")
    device = lax.axis_index("mem")
    slot_count = TASK_DEV
    own_amp = amplitudes[0, 0]
    swapped = lax.all_to_all(own_amp, "grp", split_axis=0, concat_axis=0, tiled=True)
    mixed_tile = (2.0 * own_amp.astype(jnp.float32) - swapped.astype(jnp.float32)).astype(
        jnp.bfloat16
    )
    own_int = integrals[0, 0]
    holders = jnp.take(owner_map, task_list[0], axis=0)
    live_all = jnp.arange(slot_count, dtype=jnp.int32)[None, :] < task_counts[0][:, None]
    got_mixed, got_int = (
        lax.all_gather(mixed_tile[None], "mem", axis=0, tiled=True),
        lax.all_gather(own_int[None], "mem", axis=0, tiled=True),
    )
    flat_live = live_all.reshape(-1)
    mine = flat_live & (holders[:, 0] == device)
    order = jnp.argsort(jnp.where(mine, 0, 1).astype(jnp.int32), stable=True)
    total_mine = jnp.sum(mine.astype(jnp.int32))
    block_size = math.gcd(members * slot_count, 16)
    block_count = (total_mine + block_size - 1) // block_size
    slot_index = jnp.arange(block_size, dtype=jnp.int32)

    def owner_step(state):
        turn, per_exec = state
        first = turn * block_size
        chosen = lax.dynamic_slice_in_dim(order, first, block_size, 0)
        picked = jnp.take(holders, chosen, axis=0)
        living = slot_index + first < total_mine
        product = block_products(got_mixed, got_int, picked, living)
        return (turn + 1, add_targets(per_exec, chosen // slot_count, living, product))

    start_exec = jnp.zeros((members, tile_order, tile_order), jnp.float32)
    _, per_exec = lax.while_loop(
        lambda state: state[0] < block_count, owner_step, (jnp.int32(0), start_exec)
    )
    summed = jnp.sum(per_exec.astype(jnp.bfloat16), axis=0, dtype=jnp.float32)
    return summed.astype(jnp.bfloat16)[None, None]


MESH = pl.DeviceIdType.MESH
STEP = 128
BAND = 32
PIECE = 2 * BAND
VMEM_BYTES = 65280 * 1024


def remote(src, dst, send_sem, recv_sem, **place):
    return pltpu.make_async_remote_copy(
        src_ref=src, dst_ref=dst, send_sem=send_sem, recv_sem=recv_sem,
        device_id=place, device_id_type=MESH,
    )


def spread_counts(members, tasks, counts, owner):
    total = tasks.shape[-1]
    slots = total // members
    ids = [tasks[field] for field in range(3)]
    rows = [jnp.zeros((1, total), jnp.int32) for _ in range(3)]
    for tile_id in range(members):
        row = owner[tile_id]
        rows = [jnp.where(ids[f] == tile_id, row, rows[f]) for f in range(3)]
    place = lax.broadcasted_iota(jnp.int32, (1, total), 1)
    live = jnp.zeros((1, total), jnp.int32)
    for executor in range(members):
        offset = place - executor * slots
        inside = (offset >= 0) & (offset < jnp.minimum(counts[0, executor], slots))
        live = jnp.where(inside, 1, live)
    key = rows[0] * members + rows[1]
    key = jnp.where(live == 1, key, -1)
    tall, wide = members * members * BAND, members * BAND
    hot_left = lax.broadcasted_iota(jnp.int32, (tall, total), 0) // BAND == key
    hot_right = lax.broadcasted_iota(jnp.int32, (wide, total), 0) // BAND == rows[2]
    spread = lax.dot_general(
        jnp.where(hot_left, 1.0, 0.0).astype(jnp.bfloat16),
        jnp.where(hot_right, 1.0, 0.0).astype(jnp.bfloat16),
        (((1,), (1,)), ((), ())),
        preferred_element_type=jnp.float32,
    )
    down = lax.broadcasted_iota(jnp.int32, (tall, wide), 0) % BAND
    across = lax.broadcasted_iota(jnp.int32, (tall, wide), 1) % BAND
    return jnp.where(down == across, spread, 0.0).astype(jnp.bfloat16)


def cycle_kernel(
    groups, members,
    amp_hbm, integ, tasks_hbm, counts_hbm, owner_hbm, out,
    amp, tasks, counts, owner,
    swap, halves, mixed_t, got_t, weighed, given, taken, kept, final, landed, passing, spread,
    swap_ss, swap_rs, int_ss, int_rs, mix_ss, mix_rs, part_ss, part_rs, out_ss, out_rs, pass_ss, pass_rs, local_sem,
):
    grp, mem = lax.axis_index("grp"), lax.axis_index("mem")
    tile = amp.shape[-1]
    half, block, rounds, planes = tile // 2, tile // groups, tile // STEP, members // 2
    pieces = half // PIECE
    plane, side = lax.div(mem, 2), lax.rem(mem, 2)
    partner = mem + 1 - 2 * side
    work_plane = planes // 2 - 1 + lax.rem(grp, 2)
    works = plane == work_plane
    outer_plane = lax.rem(grp, 2) * (planes - 1)
    adds = plane == outer_plane
    own_rows = pl.ds(pl.multiple_of(side * half, half), half)

    amp_in = pltpu.make_async_copy(amp_hbm, amp, local_sem.at[0])
    tasks_in = pltpu.make_async_copy(tasks_hbm, tasks, local_sem.at[1])
    counts_in = pltpu.make_async_copy(counts_hbm, counts, local_sem.at[2])
    owner_in = pltpu.make_async_copy(owner_hbm, owner, local_sem.at[3])
    half_in = pltpu.make_async_copy(integ.at[0, 0, own_rows], halves.at[mem], local_sem.at[4])
    amp_in.start()

    @pl.when(works)
    def _():
        tasks_in.start()
        counts_in.start()
        owner_in.start()
        half_in.start()

    barrier = pltpu.get_barrier_semaphore()
    for turn in range(1, groups):
        pl.semaphore_signal(
            barrier, inc=1, device_id={"grp": lax.rem(grp + turn, groups)}, device_id_type=MESH
        )

    @pl.when(works)
    def _():
        for turn in range(1, members):
            pl.semaphore_signal(
                barrier, inc=1, device_id={"mem": lax.rem(mem + turn, members)}, device_id_type=MESH
            )
        pl.semaphore_wait(barrier, groups + members - 2)

    @pl.when(jnp.logical_not(works))
    def _():
        for worker_side in range(2):
            pl.semaphore_signal(
                barrier, inc=1, device_id={"mem": work_plane * 2 + worker_side}, device_id_type=MESH
            )
        pl.semaphore_signal(barrier, inc=1, device_id={"mem": partner}, device_id_type=MESH)
        pl.semaphore_wait(barrier, groups + 2)

    def swap_copy(peer):
        return remote(
            amp_hbm.at[0, 0, pl.ds(pl.multiple_of(peer * block, block), block)],
            swap.at[grp], swap_ss.at[peer], swap_rs.at[grp], grp=peer,
        )

    def int_copy(piece, worker_side):
        return remote(
            integ.at[0, 0, pl.ds(worker_side * half + piece * PIECE, PIECE)],
            halves.at[mem, pl.ds(piece * PIECE, PIECE)],
            int_ss.at[piece, worker_side], int_rs.at[piece, mem],
            mem=work_plane * 2 + worker_side,
        )

    def mix_copy(turn, worker_side):
        return remote(
            mixed_t.at[turn, pl.ds(worker_side * half, half)],
            got_t.at[turn, mem], mix_ss.at[turn, worker_side], mix_rs.at[turn, mem],
            mem=work_plane * 2 + worker_side,
        )

    def part_copy(turn, row):
        return remote(
            given.at[turn, row], taken.at[turn, row],
            part_ss.at[turn, row], part_rs.at[turn, row], mem=partner,
        )

    def outer_copy(turn, kind):
        return remote(
            final.at[turn, outer_plane] if kind == 0 else given.at[turn, outer_plane],
            landed.at[turn, side] if kind == 0 else passing.at[turn],
            pass_ss.at[turn, kind], pass_rs.at[turn, side if kind == 0 else 2],
            mem=outer_plane * 2 + side,
        )

    def pass_copy(turn):
        return remote(
            passing.at[turn], landed.at[turn, side],
            pass_ss.at[turn, 0], pass_rs.at[turn, side], mem=partner,
        )

    def out_copy(turn, row):
        return remote(
            final.at[turn, row], out.at[0, 0, pl.ds(turn * STEP, STEP)],
            out_ss.at[turn, row], out_rs.at[turn], mem=row * 2 + side,
        )

    def own_copy(turn):
        return pltpu.make_async_copy(
            final.at[turn, plane], out.at[0, 0, pl.ds(turn * STEP, STEP)], out_rs.at[turn],
        )

    def to_workers(do):
        for worker_side in range(2):
            @pl.when(mem != work_plane * 2 + worker_side)
            def _():
                do(worker_side)

    for turn in range(1, groups):
        swap_copy(lax.rem(grp + turn, groups)).start()
    for piece in range(pieces):
        to_workers(lambda worker_side: int_copy(piece, worker_side).start())

    amp_in.wait()
    own_block = pl.ds(pl.multiple_of(grp * block, block), block)
    swap[grp] = amp[0, 0, own_block]

    for turn in range(1, groups):
        peer = lax.rem(grp + turn, groups)
        remote(
            swap.at[peer], swap.at[peer], swap_ss.at[peer], swap_rs.at[peer], grp=peer
        ).wait_recv()
    for turn in range(rounds):
        rows = pl.ds(turn * STEP, STEP)
        swapped = swap[...].reshape(tile, tile)[turn * STEP : (turn + 1) * STEP]
        mixed = (
            2.0 * amp[0, 0, rows].astype(jnp.float32) - swapped.astype(jnp.float32)
        )
        mixed_t[turn] = mixed.T.astype(jnp.bfloat16)
        to_workers(lambda worker_side: mix_copy(turn, worker_side).start())

        @pl.when(works)
        def _():
            got_t[turn, mem] = mixed_t[turn, own_rows]

    @pl.when(works)
    def _():
        tasks_in.wait()
        counts_in.wait()
        owner_in.wait()
        half_in.wait()
        spread[...] = spread_counts(members, tasks, counts, owner)
        for piece in range(pieces):
            first = piece * PIECE
            for source in range(members):
                @pl.when(mem != source)
                def _():
                    arrived = halves.at[source, pl.ds(first, PIECE)]
                    remote(
                        arrived, arrived, int_ss.at[0, 0], int_rs.at[piece, source], mem=partner
                    ).wait_recv()
            bands = [
                halves[:, pl.ds(first + band * BAND, BAND)].reshape(members * BAND, tile)
                for band in range(2)
            ]
            sums = jnp.dot(
                spread[...], jnp.concatenate(bands, axis=1), preferred_element_type=jnp.float32
            ).astype(jnp.bfloat16)
            for band in range(2):
                rows = pl.ds(first + band * BAND, BAND)
                for target in range(members):
                    high = members * BAND
                    weighed[target % 2, :, rows, pl.ds(target // 2 * tile, tile)] = sums[
                        target * high : (target + 1) * high, band * tile : (band + 1) * tile
                    ].reshape(members, BAND, tile)

        def finish(turn):
            for row in range(planes):
                @pl.when(outer_plane != row)
                def _():
                    part_copy(turn, row).wait_recv()
                    final[turn, row] = (
                        kept[turn, row] + taken[turn, row].astype(jnp.float32)
                    ).astype(jnp.bfloat16)

                @pl.when((outer_plane != row) & (plane != row))
                def _():
                    out_copy(turn, row).start()

                @pl.when(plane == row)
                def _():
                    own_copy(turn).start()

        for turn in range(rounds):
            for source in range(members):
                @pl.when(mem != source)
                def _():
                    remote(
                        got_t.at[turn, source], got_t.at[turn, source],
                        mix_ss.at[turn, 0], mix_rs.at[turn, source], mem=partner,
                    ).wait_recv()
            left = got_t[turn].reshape(members * half, STEP).T

            def multiply(target_side, pair):
                wide = 2 * tile
                right = weighed[target_side, :, :, pl.ds(pair * wide, wide)]
                both = jnp.dot(
                    left, right.reshape(members * half, wide), preferred_element_type=jnp.float32
                )
                return [(pair * 2, both[:, :tile]), (pair * 2 + 1, both[:, tile:])]

            for pair in range(planes // 2):
                for row, product in multiply(1 - side, pair):
                    given[turn, row] = product.astype(jnp.bfloat16)

                    @pl.when(outer_plane == row)
                    def _():
                        outer_copy(turn, 1).start()

                    @pl.when(outer_plane != row)
                    def _():
                        part_copy(turn, row).start()
            for pair in range(planes // 2):
                for row, product in multiply(side, pair):
                    kept[turn, row] = product

                    @pl.when(outer_plane == row)
                    def _():
                        final[turn, row] = kept[turn, row].astype(jnp.bfloat16)
                        outer_copy(turn, 0).start()

            if turn:
                finish(turn - 1)
        finish(rounds - 1)
        for turn in range(rounds):
            own_copy(turn).wait()
            for kind in range(2):
                outer_copy(turn, kind).wait_send()
            for row in range(planes):
                @pl.when(outer_plane != row)
                def _():
                    part_copy(turn, row).wait_send()

                @pl.when((outer_plane != row) & (plane != row))
                def _():
                    out_copy(turn, row).wait_send()

    @pl.when(jnp.logical_not(works | adds))
    def _():
        for turn in range(rounds):
            out_copy(turn, 0).wait_recv()

    @pl.when(adds)
    def _():
        def pass_arrival(turn, kind):
            target = passing.at[turn] if kind == 2 else landed.at[turn, kind]
            return remote(
                target, target, pass_ss.at[turn, 0], pass_rs.at[turn, kind], mem=partner
            )

        def add(turn):
            for worker_side in range(2):
                pass_arrival(turn, worker_side).wait_recv()
            final[turn, plane] = (
                landed[turn, 0].astype(jnp.float32) + landed[turn, 1].astype(jnp.float32)
            ).astype(jnp.bfloat16)
            own_copy(turn).start()

        for turn in range(rounds):
            pass_arrival(turn, 2).wait_recv()
            pass_copy(turn).start()
            if turn:
                add(turn - 1)
        add(rounds - 1)
        for turn in range(rounds):
            pass_copy(turn).wait_send()
            own_copy(turn).wait()

    for turn in range(1, groups):
        swap_copy(lax.rem(grp + turn, groups)).wait_send()
    for piece in range(pieces):
        to_workers(lambda worker_side: int_copy(piece, worker_side).wait_send())
    for turn in range(rounds):
        to_workers(lambda worker_side: mix_copy(turn, worker_side).wait_send())


def local_workers(amplitudes, integrals, task_list, task_counts, owner_map):
    groups, members = lax.axis_size("grp"), lax.axis_size("mem")
    tile = amplitudes.shape[-1]
    half, rounds, planes = tile // 2, tile // STEP, members // 2
    hbm = pl.BlockSpec(memory_space=pltpu.HBM)
    dma = pltpu.SemaphoreType.DMA
    bf16 = jnp.bfloat16
    return pl.pallas_call(
        functools.partial(cycle_kernel, groups, members),
        out_shape=jax.ShapeDtypeStruct(amplitudes.shape, bf16),
        in_specs=[hbm] * 5,
        out_specs=hbm,
        scratch_shapes=[
            pltpu.VMEM(amplitudes.shape, bf16),
            pltpu.VMEM((3, 1, task_list.shape[1]), jnp.int32),
            pltpu.SMEM(task_counts.shape, jnp.int32),
            pltpu.SMEM(owner_map.shape, jnp.int32),
            pltpu.VMEM((groups, tile // groups, tile), bf16),
            pltpu.VMEM((members, half, tile), bf16),
            pltpu.VMEM((rounds, tile, STEP), bf16),
            pltpu.VMEM((rounds, members, half, STEP), bf16),
            pltpu.VMEM((2, members, half, planes * tile), bf16),
            pltpu.VMEM((rounds, planes, STEP, tile), bf16),
            pltpu.VMEM((rounds, planes, STEP, tile), bf16),
            pltpu.VMEM((rounds, planes, STEP, tile), jnp.float32),
            pltpu.VMEM((rounds, planes, STEP, tile), bf16),
            pltpu.VMEM((rounds, 2, STEP, tile), bf16),
            pltpu.VMEM((rounds, STEP, tile), bf16),
            pltpu.VMEM((members * members * BAND, members * BAND), bf16),
            dma((groups,)), dma((groups,)),
            dma((half // PIECE, 2)), dma((half // PIECE, members)),
            dma((rounds, 2)), dma((rounds, members)),
            dma((rounds, planes)), dma((rounds, planes)),
            dma((rounds, planes)), dma((rounds,)),
            dma((rounds, 2)), dma((rounds, 3)),
            dma((5,)),
        ],
        compiler_params=pltpu.CompilerParams(
            collective_id=0, has_side_effects=True, vmem_limit_bytes=VMEM_BYTES
        ),
    )(amplitudes, integrals, jnp.transpose(task_list, (2, 0, 1)), task_counts, owner_map)


def solution(mesh):
    placed = (
        P("grp", "mem", None, None),
        P("grp", "mem", None, None),
        P("grp", None, None),
        P("grp", None),
        P(),
    )
    body = local_workers if mesh.shape["mem"] == 2 * 4 else local
    return jax.shard_map(
        body, mesh=mesh, in_specs=placed, out_specs=P("grp", "mem", None, None), check_vma=False
    )
```
